32 devices in a mesh: seq: 8 (over y, x, core), head: 4 (over z).
Axes of the slice: x: 2, y: 2, z: 4, core: 2. Of those that a mesh axis runs over, the one named last changes fastest.
Arguments:
- queries: bfloat16 [2048, 8192], P(('seq', 'head')), may hold values from -0.125 to 0.125
- key_rows: bfloat16 [2048, 8192], P(('seq', 'head')), may hold values from -0.125 to 0.125
- value_rows: bfloat16 [2048, 8192], P(('seq', 'head')), may hold values from -0.125 to 0.125
- out_grad: bfloat16 [2048, 8192], P(('seq', 'head')), may hold values from -6 to 6
- log_decay: float32 [64, 2048], P('head', 'seq'), may hold values from -0.9 to 0, as said below
Outputs:
- query_grad: bfloat16 [2048, 8192], P(('seq', 'head'))
- key_grad: bfloat16 [2048, 8192], P(('seq', 'head'))
- value_grad: bfloat16 [2048, 8192], P(('seq', 'head'))
The draws below stay inside these ranges and needn't reach their ends.
Inputs may be any that keep to these rules, and one draw needn't show every extreme that they name: `log_decay`: never positive.
All inputs are finite; a program needn't handle non-finite values.
Results may differ from the reference program's by a relative error of at most 0.0057.
Values may be sent and summed in bfloat16 or wider, within the bound.
No kernel may reach another device: no remote copies, remote signals or barrier semaphores. Data moves between devices by JAX's collectives and lax.ppermute only.
A program may use at most 128 MiB of HBM per device.

```python
import jax
import jax.numpy as jnp
from jax import lax

HEAD_COUNT = 64
HEAD_DIM = 128
BLOCK = 256
SEG_DEV = 256
TOKEN_COUNT = 2048


def draw_log_decay(key, part):
    every_key = jax.random.split(key, 7)
    fast_share = 0.5
    fast_heads = jax.random.uniform(every_key[0], (HEAD_COUNT, 1)) < fast_share
    fast_rate = jax.random.uniform(every_key[1], (HEAD_COUNT, 1), jnp.float32, 1.0 / 50.0, 1.0 / 30.0)
    slow_rate = jax.random.uniform(every_key[2], (HEAD_COUNT, 1), jnp.float32, 0.25, 1.0) * 0.5 / TOKEN_COUNT
    head_decay_rate = jnp.where(fast_heads, fast_rate, slow_rate)
    coarse_estimate = jnp.exp(jax.random.uniform(every_key[3], (HEAD_COUNT, TOKEN_COUNT), jnp.float32, -0.69, 0.69))
    regions = TOKEN_COUNT // SEG_DEV
    segment_multiplier = jnp.exp(jax.random.uniform(every_key[4], (HEAD_COUNT, regions, 1), jnp.float32, -0.69, 0.69))
    segment_multiplier = jnp.broadcast_to(segment_multiplier, (HEAD_COUNT, regions, SEG_DEV)).reshape(HEAD_COUNT, TOKEN_COUNT)
    spike_position = jax.random.randint(every_key[5], (HEAD_COUNT, 2), 0, TOKEN_COUNT)
    token_positions = jnp.arange(TOKEN_COUNT)
    spike_applied = jnp.any(token_positions[None, :, None] == spike_position[:, None, :], axis=-1)
    spike_magnitude = jax.random.uniform(every_key[6], (HEAD_COUNT, TOKEN_COUNT), jnp.float32, 0.2, 0.5)
    spike_log_decay = jnp.where(spike_applied, jnp.log(1.0 - spike_magnitude), 0.0)
    return (-head_decay_rate * coarse_estimate * segment_multiplier + spike_log_decay).astype(jnp.float32)


def levels(stream_key, dims, cuts, low, high):
    factor_of = 1.0
    for dim, parts in cuts:
        steps = jax.random.uniform(jax.random.fold_in(jax.random.fold_in(stream_key, 6), dim), (parts,), jnp.float32, low / len(cuts), high / len(cuts))
        factor_of = factor_of * jnp.repeat(jnp.exp(steps), dims[dim] // parts).reshape((-1,) + (1,) * (len(dims) - 1 - dim))
    return factor_of


def centred(own_key, extent, scale, most, cuts=(), kind=jnp.bfloat16):
    values = jax.random.normal(own_key, extent, jnp.float32) * scale
    if len(cuts) > 0:
        values = levels(own_key, extent, cuts, -0.22, 0.18) * values
    return jnp.clip(values, min=-most, max=most).astype(kind)


def setup_inputs(seed: int = 0) -> dict:
    splits = jax.random.split(jax.random.key(seed), 6)
    queries = centred(splits[0], (TOKEN_COUNT, HEAD_COUNT * HEAD_DIM), (16 * HEAD_DIM) ** -0.5, 0.125, ((0, 32),))
    key_rows = centred(splits[1], (TOKEN_COUNT, HEAD_COUNT * HEAD_DIM), (16 * HEAD_DIM) ** -0.5, 0.125, ((0, 32),))
    value_rows = centred(splits[2], (TOKEN_COUNT, HEAD_COUNT * HEAD_DIM), (16 * HEAD_DIM) ** -0.5, 0.125, ((0, 32),))
    out_grad = centred(splits[3], (TOKEN_COUNT, HEAD_COUNT * HEAD_DIM), 1.0, 6.0, ((0, 32),))
    log_decay = draw_log_decay(jax.random.fold_in(splits[5], 71), 0)
    return dict(queries=queries, key_rows=key_rows, value_rows=value_rows, out_grad=out_grad, log_decay=log_decay)


def as_float(array):
    return array.astype(jnp.float32)


def scaled_rows(rows, weight):
    return (rows.astype(jnp.float32) * weight[..., None]).astype(jnp.bfloat16)


def one_head(operands):
    query_block, key_block, value_block, grad_block, decay_row = operands
    nblocks = TOKEN_COUNT // BLOCK
    query_block = query_block.reshape(nblocks, BLOCK, HEAD_DIM)
    key_block = key_block.reshape(nblocks, BLOCK, HEAD_DIM)
    value_block = value_block.reshape(nblocks, BLOCK, HEAD_DIM)
    grad_block = grad_block.reshape(nblocks, BLOCK, HEAD_DIM)
    cumulative = jnp.cumsum(decay_row.reshape(nblocks, BLOCK), axis=1)
    last_value = cumulative[:, -1:]
    query_weight = jnp.exp(cumulative)
    key_weight = jnp.exp(last_value - cumulative)
    block_gate = jnp.exp(last_value[:, 0])
    key_scaled = scaled_rows(key_block, key_weight)
    query_scaled = scaled_rows(query_block, query_weight)
    block_state = jnp.einsum("nbi,nbj->nij", as_float(key_scaled), as_float(value_block))
    block_grad = jnp.einsum("nbi,nbj->nij", as_float(query_scaled), as_float(grad_block))

    def advance(running, element):
        gate_now, state_now = element
        return gate_now * running + state_now, running

    zero_state = jnp.zeros((HEAD_DIM, HEAD_DIM), jnp.float32)
    _, state_in = lax.scan(advance, zero_state, (block_gate, block_state))
    _, state_out = lax.scan(advance, zero_state, (block_gate, block_grad), reverse=True)
    state_in_low = state_in.astype(jnp.bfloat16)
    state_out_low = state_out.astype(jnp.bfloat16)
    token_positions = jnp.arange(BLOCK)
    causal = token_positions[:, None] >= token_positions[None, :]
    spread_log = cumulative[:, :, None] - cumulative[:, None, :]
    decay_matrix = jnp.where(causal, jnp.exp(jnp.where(causal, spread_log, 0.0)), 0.0)
    grad_scores = (jnp.einsum("nti,nsi->nts", as_float(grad_block), as_float(value_block)) * decay_matrix).astype(jnp.bfloat16)
    scores = (jnp.einsum("nti,nsi->nts", as_float(query_block), as_float(key_block)) * decay_matrix).astype(jnp.bfloat16)
    query_grad = jnp.einsum("nts,nsi->nti", as_float(grad_scores), as_float(key_block))
    query_grad = query_grad + query_weight[..., None] * jnp.einsum("ntj,nij->nti", as_float(grad_block), as_float(state_in_low))
    key_grad = jnp.einsum("nts,nti->nsi", as_float(grad_scores), as_float(query_block))
    key_grad = key_grad + key_weight[..., None] * jnp.einsum("nsj,nij->nsi", as_float(value_block), as_float(state_out_low))
    value_grad = jnp.einsum("nts,ntj->nsj", as_float(scores), as_float(grad_block))
    value_grad = value_grad + key_weight[..., None] * jnp.einsum("nsi,nij->nsj", as_float(key_block), as_float(state_out_low))
    return (query_grad.reshape(TOKEN_COUNT, HEAD_DIM).astype(jnp.bfloat16),
            key_grad.reshape(TOKEN_COUNT, HEAD_DIM).astype(jnp.bfloat16),
            value_grad.reshape(TOKEN_COUNT, HEAD_DIM).astype(jnp.bfloat16))


def by_head(array):
    return array.reshape(TOKEN_COUNT, HEAD_COUNT, HEAD_DIM).transpose(1, 0, 2)


def by_token(array):
    return array.transpose(1, 0, 2).reshape(TOKEN_COUNT, HEAD_COUNT * HEAD_DIM)


def reference(queries, key_rows, value_rows, out_grad, log_decay):
    query_grad, key_grad, value_grad = lax.map(
        one_head, (by_head(queries), by_head(key_rows), by_head(value_rows), by_head(out_grad), log_decay))
    return (by_token(query_grad), by_token(key_grad), by_token(value_grad))
```

```python
import functools

import jax
import jax.numpy as jnp
from jax import lax
from jax.experimental import pallas as pl
from jax.experimental.pallas import tpu as pltpu
from jax.sharding import PartitionSpec as P

HEAD_DIM = 128
PARTS = (4, 2)
VMEM = 48 * 1024 * 1024


def swap(x, axis, bit):
    return lax.ppermute(x, axis, [(i, i ^ bit) for i in range(lax.axis_size(axis))])


def params():
    return pltpu.CompilerParams(vmem_limit_bytes=VMEM)


def cost(flops, bytes_accessed):
    return pl.CostEstimate(flops=flops, bytes_accessed=bytes_accessed, transcendentals=0)


def dot(a, b, dims):
    return lax.dot_general(a, b, (dims, ((), ())), preferred_element_type=jnp.float32)


NN = ((1,), (0,))
NT = ((1,), (1,))
TN = ((0,), (0,))


def head_cols(h):
    return slice(h * HEAD_DIM, (h + 1) * HEAD_DIM)


def pack_kernel(cols_ref, q_ref, k_ref, v_ref, g_ref, out_ref):
    for a, ref in enumerate((q_ref, k_ref, v_ref, g_ref)):
        out_ref[0, a] = ref[...]


def pack(cols, arrays, hw, hb):
    rows = arrays[0].shape[0]
    width = hb * HEAD_DIM
    steps = hw // hb
    block = pl.BlockSpec((rows, width), lambda o, i, c: (0, c[o] + i))
    return pl.pallas_call(
        pack_kernel,
        grid_spec=pltpu.PrefetchScalarGridSpec(
            num_scalar_prefetch=1,
            grid=(2, steps),
            in_specs=[block] * 4,
            out_specs=pl.BlockSpec((1, 4, rows, width), lambda o, i, c: (o, 0, 0, i)),
        ),
        out_shape=jax.ShapeDtypeStruct((2, 4, rows, hw * HEAD_DIM), jnp.bfloat16),
        compiler_params=params(),
        cost_estimate=cost(0, 4 * 8 * rows * hw * HEAD_DIM),
        name="pack",
    )(cols, *arrays)


def states_kernel(half, hb, cols_ref, *refs):
    raw = (refs[:4], refs[4:8])
    recv = refs[8 : 8 + half - 1]
    qw_ref, kw_ref, own_ref, send_ref = refs[8 + half - 1 :]
    for o in range(2):
        for h in range(hb):
            c = head_cols(h)

            def rows(a):
                pieces = [raw[o][a][:, c]] + [r[o, a, :, c] for r in recv]
                return jnp.concatenate(pieces, axis=0) if len(pieces) > 1 else pieces[0]

            qw = qw_ref[0, o, :, h : h + 1]
            kw = kw_ref[0, o, :, h : h + 1]
            ks = (rows(1).astype(jnp.float32) * kw).astype(jnp.bfloat16)
            qs = (rows(0).astype(jnp.float32) * qw).astype(jnp.bfloat16)
            state = dot(ks, rows(2), TN)
            grad = dot(qs, rows(3), TN)
            if o == 0:
                own_ref[0, h] = state
                own_ref[1, h] = grad
            else:
                send_ref[0, h] = state.astype(jnp.bfloat16)
                send_ref[1, h] = grad.astype(jnp.bfloat16)


def block_states(cols, arrays, recv, qw, kw, hw, hb):
    rows = arrays[0].shape[0]
    half = len(recv) + 1
    width = hb * HEAD_DIM
    steps = hw // hb
    own_block = pl.BlockSpec((rows, width), lambda i, c: (0, c[0] + i))
    mirror_block = pl.BlockSpec((rows, width), lambda i, c: (0, c[1] + i))
    recv_block = pl.BlockSpec((2, 4, rows, width), lambda i, c: (0, 0, 0, i))
    weight_block = pl.BlockSpec((1, 2, half * rows, hb), lambda i, c: (i, 0, 0, 0))
    state_block = pl.BlockSpec((2, hb, HEAD_DIM, HEAD_DIM), lambda i, c: (0, i, 0, 0))
    shape = (2, hw, HEAD_DIM, HEAD_DIM)
    return pl.pallas_call(
        functools.partial(states_kernel, half, hb),
        grid_spec=pltpu.PrefetchScalarGridSpec(
            num_scalar_prefetch=1,
            grid=(steps,),
            in_specs=[own_block] * 4
            + [mirror_block] * 4
            + [recv_block] * (half - 1)
            + [weight_block] * 2,
            out_specs=[state_block, state_block],
        ),
        out_shape=[
            jax.ShapeDtypeStruct(shape, jnp.float32),
            jax.ShapeDtypeStruct(shape, jnp.bfloat16),
        ],
        compiler_params=params(),
        cost_estimate=cost(
            hw * 2 * 4 * half * rows * HEAD_DIM * HEAD_DIM, 16 * half * rows * hw * HEAD_DIM
        ),
        name="states",
    )(cols, *arrays, *arrays, *recv, qw, kw)


def grads_kernel(half, hb, aliased, cols_ref, *refs):
    raw = refs[:4]
    recv = refs[4 : 4 + half - 1]
    rest = refs[4 + half - 1 :]
    qw_ref, kw_ref, cumc_ref, cumr_ref, bias_ref, st_ref = rest[:6]
    rest = rest[6 + (3 if aliased else 0) :]
    outs = rest[:3]
    sends = rest[3:]
    n = raw[0].shape[0]
    bias = bias_ref[...]
    for h in range(hb):
        c = head_cols(h)

        def rows(a):
            pieces = [raw[a][:, c]] + [r[0, a, :, c] for r in recv]
            return jnp.concatenate(pieces, axis=0) if len(pieces) > 1 else pieces[0]

        q, k, v, g = rows(0), rows(1), rows(2), rows(3)
        qw = qw_ref[0, :, h : h + 1]
        kw = kw_ref[0, :, h : h + 1]
        decay = jnp.exp(cumc_ref[0, :, h : h + 1] - cumr_ref[0, h : h + 1, :] + bias)
        gs = (dot(g, v, NT) * decay).astype(jnp.bfloat16)
        sc = (dot(q, k, NT) * decay).astype(jnp.bfloat16)
        forward = st_ref[0, h]
        backward = st_ref[1, h]
        dq = dot(gs, k, NN) + qw * dot(g, forward, NT)
        dk = dot(gs, q, TN) + kw * dot(v, backward, NT)
        dv = dot(sc, g, TN) + kw * dot(k, backward, NN)
        for a, result in enumerate((dq, dk, dv)):
            result = result.astype(jnp.bfloat16)
            outs[a][:, c] = result[:n]
            for m, send in enumerate(sends):
                send[a, :, c] = result[(m + 1) * n : (m + 2) * n]


def grads(cols, arrays, recv, group, weights, states, outs, hw, hb):
    rows, full = arrays[0].shape
    half = len(recv) + 1
    span = half * rows
    width = hb * HEAD_DIM
    steps = hw // hb
    qw, kw, cumc, cumr, bias = weights
    raw_block = pl.BlockSpec((rows, width), lambda i, c: (0, c[group] + i))
    recv_block = pl.BlockSpec((1, 4, rows, width), lambda i, c: (group, 0, 0, i))
    column = pl.BlockSpec((1, span, hb), lambda i, c: (i, 0, 0))
    row = pl.BlockSpec((1, hb, span), lambda i, c: (i, 0, 0))
    whole = pl.BlockSpec((span, span), lambda i, c: (0, 0))
    state_block = pl.BlockSpec((2, hb, HEAD_DIM, HEAD_DIM), lambda i, c: (0, i, 0, 0))
    aliased = outs is not None
    first = 1 + 4 + (half - 1) + 6
    operands = (cols, *arrays, *recv, qw, kw, cumc, cumr, bias, states)
    results = pl.pallas_call(
        functools.partial(grads_kernel, half, hb, aliased),
        grid_spec=pltpu.PrefetchScalarGridSpec(
            num_scalar_prefetch=1,
            grid=(steps,),
            in_specs=[raw_block] * 4
            + [recv_block] * (half - 1)
            + [column] * 3
            + [row, whole, state_block]
            + ([pl.BlockSpec(memory_space=pl.ANY)] * 3 if aliased else []),
            out_specs=[raw_block] * 3
            + [pl.BlockSpec((3, rows, width), lambda i, c: (0, 0, i))] * (half - 1),
        ),
        out_shape=[jax.ShapeDtypeStruct((rows, full), jnp.bfloat16)] * 3
        + [jax.ShapeDtypeStruct((3, rows, hw * HEAD_DIM), jnp.bfloat16)] * (half - 1),
        input_output_aliases={first + a: a for a in range(3)} if aliased else {},
        compiler_params=params(),
        cost_estimate=cost(
            hw * 2 * (5 * span * span * HEAD_DIM + 3 * span * HEAD_DIM * HEAD_DIM),
            14 * span * hw * HEAD_DIM,
        ),
        name="grads",
    )(*operands, *(outs if aliased else ()))
    return (results[:3], results[3:])


def place_kernel(cols_ref, part_ref, *refs):
    for a in range(3):
        refs[3 + a][...] = part_ref[a]


def place(cols, group, part, outs, hw, hb):
    rows, full = outs[0].shape
    width = hb * HEAD_DIM
    return pl.pallas_call(
        place_kernel,
        grid_spec=pltpu.PrefetchScalarGridSpec(
            num_scalar_prefetch=1,
            grid=(hw // hb,),
            in_specs=[pl.BlockSpec((3, rows, width), lambda i, c: (0, 0, i))]
            + [pl.BlockSpec(memory_space=pl.ANY)] * 3,
            out_specs=[pl.BlockSpec((rows, width), lambda i, c: (0, c[group] + i))] * 3,
        ),
        out_shape=[jax.ShapeDtypeStruct((rows, full), jnp.bfloat16)] * 3,
        input_output_aliases={2 + a: a for a in range(3)},
        compiler_params=params(),
        cost_estimate=cost(0, 12 * rows * hw * HEAD_DIM),
        name="place",
    )(cols, part, *outs)


def seq_logs(block_log):
    every = block_log[None]
    place_ = lax.axis_index("seq")
    bit = 1
    while bit < lax.axis_size("seq"):
        other = swap(every, "seq", bit)
        mine_late = (place_ & bit) != 0
        every = jnp.where(
            mine_late,
            jnp.concatenate([other, every], axis=0),
            jnp.concatenate([every, other], axis=0),
        )
        bit *= 2
    return every


def scan_weights(every):
    peers = lax.axis_size("seq")
    me = lax.axis_index("seq")
    index = jnp.arange(peers)[:, None]

    def total(low, high):
        inside = (index >= low) & (index < high)
        return jnp.exp(jnp.sum(jnp.where(inside, every, 0.0), axis=0))

    result = []
    bit = 1
    while bit < peers:
        start = me - me % bit
        other = start ^ bit
        mine, theirs = total(start, start + bit), total(other, other + bit)
        result.append((total(start, me), total(me + 1, start + bit), mine, theirs))
        bit *= 2
    return result


def spread(gate):
    return gate[:, None, None]


def seq_scan(state_total, grad_total, weights):
    peers = lax.axis_size("seq")
    me = lax.axis_index("seq")
    before = jnp.zeros_like(state_total)
    after = jnp.zeros_like(grad_total)
    for level, (early, late, mine, theirs) in enumerate(weights):
        bit = 1 << level
        upper = (me & bit) != 0
        early = spread(jnp.where(upper, early, 0.0))
        late = spread(jnp.where(upper, 0.0, late))
        if 2 * bit == peers:
            other = swap(
                jnp.where(upper, grad_total, state_total).astype(jnp.bfloat16), "seq", bit
            ).astype(jnp.float32)
            before = before + early * other
            after = after + late * other
        else:
            other = swap(
                jnp.stack([state_total, grad_total]).astype(jnp.bfloat16), "seq", bit
            ).astype(jnp.float32)
            before = before + early * other[0]
            after = after + late * other[1]
            keep_state = spread(jnp.where(upper, 1.0, theirs))
            add_state = spread(jnp.where(upper, mine, 1.0))
            keep_grad = spread(jnp.where(upper, theirs, 1.0))
            add_grad = spread(jnp.where(upper, 1.0, mine))
            state_total = keep_state * state_total + add_state * other[0]
            grad_total = keep_grad * grad_total + add_grad * other[1]
    return (before, after)


def plan(heads):
    if heads % 8 == 0:
        return [(0, heads // 2), (heads // 2, heads // 2)]
    return [(0, heads)]


def local(queries, key_rows, value_rows, out_grad, log_decay):
    arrays = (queries, key_rows, value_rows, out_grad)
    rows = queries.shape[0]
    heads = log_decay.shape[0]
    n = lax.axis_size("head")
    half = n // 2
    z = lax.axis_index("head")
    slot = z % half
    low = z < half
    mirror = z ^ half
    span = half * rows

    logs = jnp.stack([log_decay, swap(log_decay, "head", half)])
    halves = logs.reshape(2, heads, 2, span)
    half_sums = jnp.sum(halves, axis=3)
    my_logs = lax.dynamic_index_in_dim(halves, z // half, axis=2, keepdims=False)
    cum = jnp.cumsum(my_logs, axis=2)
    last = cum[:, :, -1:]
    cum = cum.reshape(2, heads, half, rows)
    order = [slot ^ m for m in range(half)]
    cum = jnp.concatenate(
        [lax.dynamic_index_in_dim(cum, at, axis=2, keepdims=False) for at in order], axis=2
    )
    query_weight = jnp.exp(cum)
    key_weight = jnp.exp(last - cum)
    positions = jnp.concatenate([at * rows + jnp.arange(rows) for at in order])
    bias = jnp.where(positions[:, None] >= positions[None, :], 0.0, -1e30).astype(jnp.float32)
    gate_low = jnp.exp(half_sums[0, :, 0])
    gate_high = jnp.exp(half_sums[0, :, 1])
    weights = scan_weights(seq_logs(half_sums[0, :, 0] + half_sums[0, :, 1]))

    waves = plan(heads)
    received = []
    blocks = []
    for w0, hw in waves:
        hb = next(b for b in PARTS + (1,) if hw % b == 0 and w0 % b == 0 and heads % b == 0)

        def cols(at):
            return (jnp.stack([at, at ^ half]) * heads + w0).astype(jnp.int32) // hb

        blocks.append((hb, cols))
        got = []
        for m in range(1, half):
            got.append(swap(pack(cols(z ^ m), arrays, hw, hb), "head", m))
        received.append(got)

    outs = None
    for w, (w0, hw) in enumerate(waves):
        hb, cols = blocks[w]
        steps = hw // hb
        here = slice(w0, w0 + hw)

        def columns(x):
            x = x[:, here].reshape(2, steps, hb, span)
            return jnp.transpose(x, (1, 0, 3, 2))

        def lines(x):
            return x[:, here].reshape(2, steps, hb, span)

        qw, kw, cumc, cumr = (
            columns(query_weight),
            columns(key_weight),
            columns(cum),
            lines(cum),
        )
        own, send = block_states(cols(z), arrays, received[w], qw, kw, hw, hb)
        theirs = swap(send, "head", half).astype(jnp.float32)
        early = jnp.where(low, own, theirs)
        late = jnp.where(low, theirs, own)
        gl, gh = spread(gate_low[here]), spread(gate_high[here])
        state_total = gh * early[0] + late[0]
        grad_total = early[1] + gl * late[1]
        before, after = seq_scan(
            state_total, grad_total, [tuple(x[here] for x in level) for level in weights]
        )
        low_states = jnp.stack([before, gh * after + late[1]]).astype(jnp.bfloat16)
        high_states = jnp.stack([gl * before + early[0], after]).astype(jnp.bfloat16)
        own_states = jnp.where(low, low_states, high_states)
        mirror_states = swap(jnp.where(low, high_states, low_states), "head", half)
        for group, states in enumerate((own_states, mirror_states)):
            outs, sends = grads(
                cols(z),
                arrays,
                received[w],
                group,
                (qw[:, group], kw[:, group], cumc[:, group], cumr[group], bias),
                states,
                outs,
                hw,
                hb,
            )
            for m, part in enumerate(sends):
                part = swap(part, "head", m + 1)
                outs = place(cols(z ^ (m + 1)), group, part, outs, hw, hb)
    return tuple(outs)


def solution(mesh):
    rows = P(("seq", "head"), None)
    return jax.shard_map(
        local,
        mesh=mesh,
        in_specs=(rows, rows, rows, rows, P("head", "seq")),
        out_specs=(rows, rows, rows),
        check_vma=False,
    )
```

```python
import functools
import math

import jax
import jax.numpy as jnp
from jax import lax
from jax.experimental import pallas as pl
from jax.experimental.pallas import tpu as pltpu
from jax.sharding import PartitionSpec as P

HEAD_DIM = 128
PART = 4
STEP = 8
VMEM = 16 * 1024 * 1024
ANY = pl.BlockSpec(memory_space=pl.ANY)
FULL = pl.BlockSpec(memory_space=pltpu.VMEM)
SCALARS = pl.BlockSpec(memory_space=pltpu.SMEM)
NN = ((1,), (0,))
NT = ((1,), (1,))
TN = ((0,), (0,))
LOW = jnp.bfloat16
COST = pl.CostEstimate(flops=1, bytes_accessed=1, transcendentals=0)
WIDE = jnp.float32


def swap(x, axis, bit):
    return lax.ppermute(x, axis, [(i, i ^ bit) for i in range(lax.axis_size(axis))])


def dot(a, b, dims):
    return lax.dot_general(a, b, (dims, ((), ())), preferred_element_type=WIDE)


def head_cols(h):
    return slice(h * HEAD_DIM, (h + 1) * HEAD_DIM)


class Order:
    def __init__(self):
        self.token = None

    def call(
        self,
        kernel,
        name,
        scalars,
        inputs,
        in_specs,
        out_shape,
        out_specs,
        grid=(),
        scratch=(),
        aliases=None,
        after=(),
        vmem=VMEM,
    ):
        extra = list(after) + ([] if self.token is None else [self.token])
        n_scalars, n_in, n_out = len(scalars), len(inputs), len(out_shape)

        def body(*refs):
            first = n_scalars + n_in
            second = first + len(extra)
            kernel(*refs[:first], *refs[second : second + n_out], *refs[second + n_out + 1 :])

        *results, self.token = pl.pallas_call(
            body,
            grid_spec=pltpu.PrefetchScalarGridSpec(
                num_scalar_prefetch=n_scalars,
                grid=grid,
                in_specs=list(in_specs) + [ANY] * len(extra),
                out_specs=list(out_specs) + [ANY],
                scratch_shapes=scratch,
            ),
            out_shape=list(out_shape) + [jax.ShapeDtypeStruct((8, 128), WIDE)],
            input_output_aliases=aliases or {},
            compiler_params=pltpu.CompilerParams(vmem_limit_bytes=vmem),
            cost_estimate=COST,
            name=name,
        )(*scalars, *inputs, *extra)
        return results


def head_states(q, k, v, g, qw, kw):
    ks = (k.astype(WIDE) * kw).astype(LOW)
    qs = (q.astype(WIDE) * qw).astype(LOW)
    return dot(ks, v, TN), dot(qs, g, TN)


def head_grads(q, k, v, g, qw, kw, cumc, cumr, bias, forward, backward):
    decay = jnp.exp(cumc - cumr + bias)
    gs = (dot(g, v, NT) * decay).astype(LOW)
    sc = (dot(q, k, NT) * decay).astype(LOW)
    dq = dot(gs, k, NN) + qw * dot(g, forward, NT)
    dk = dot(gs, q, TN) + kw * dot(v, backward, NT)
    dv = dot(sc, g, TN) + kw * dot(k, backward, NN)
    return dq.astype(LOW), dk.astype(LOW), dv.astype(LOW)


def pack(order, target, arrays, hw, after=(), vmem=60 * 1024 * 1024):
    rows = arrays[0].shape[0]
    width = hw * HEAD_DIM
    groups = target.shape[0]

    def kernel(at_ref, *refs):
        ins, out, sems = refs[:4], refs[4], refs[5]
        copies = []
        for o in range(groups):
            columns = pl.ds(pl.multiple_of(at_ref[o] * HEAD_DIM, HEAD_DIM), width)
            for a, ref in enumerate(ins):
                copies.append(
                    pltpu.make_async_copy(
                        ref.at[:, columns], out.at[o, a], sems.at[len(copies)]
                    )
                )
        for copy in copies:
            copy.start()
        for copy in copies:
            copy.wait()

    (packed,) = order.call(
        kernel,
        "pack",
        [target],
        arrays,
        [pl.BlockSpec(memory_space=pltpu.HBM)] * 4,
        [jax.ShapeDtypeStruct((groups, 4, rows, width), LOW)],
        [FULL],
        scratch=[pltpu.SemaphoreType.DMA((4 * groups,))],
        after=after,
        vmem=vmem,
    )
    return packed


def decays(order, at, logs, rows, pieces, hb):
    heads, length = logs[0].shape
    span = pieces * rows
    groups = len(logs)
    steps = heads // hb

    def kernel(at_ref, *refs):
        sources = refs[:groups]
        cumr, cumc, qw, kw, bias = refs[groups:]
        slot, upper = at_ref[0], at_ref[1]

        def position(axis):
            p = lax.broadcasted_iota(jnp.int32, (span, span), axis)
            return ((p // rows) ^ slot) * rows + p % rows

        down, along = position(0), position(1)
        bias[...] = jnp.where(down >= along, 0.0, -1e30)
        source = lax.broadcasted_iota(jnp.int32, (span, span), 0)
        upto = (source <= along).astype(WIDE)
        ones = jnp.ones((span, span), WIDE)
        for o, ref in enumerate(sources):
            rows_in = ref[...]
            if span < length:
                rows_in = jnp.where(upper == 0, rows_in[:, :span], rows_in[:, span:])

            def exact(a, b, dims):
                return lax.dot_general(
                    a,
                    b,
                    (dims, ((), ())),
                    precision=lax.Precision.HIGHEST,
                    preferred_element_type=WIDE,
                )

            line = exact(rows_in, upto, NN)
            column = exact(upto, rows_in, ((0,), (1,)))
            total = exact(ones, rows_in, NT)
            query = jnp.exp(column)
            key = jnp.exp(total - column)
            for i in range(steps):
                part = slice(i * hb, (i + 1) * hb)
                cumr[i, o] = line[part]
                cumc[i, o] = column[:, part]
                qw[i, o] = query[:, part]
                kw[i, o] = key[:, part]

    columns = jax.ShapeDtypeStruct((steps, groups, span, hb), WIDE)
    return order.call(
        kernel,
        "decays",
        [at],
        logs,
        [FULL] * groups,
        [
            jax.ShapeDtypeStruct((steps, groups, hb, span), WIDE),
            columns,
            columns,
            columns,
            jax.ShapeDtypeStruct((span, span), WIDE),
        ],
        [FULL] * 5,
    )


def states(order, pieces, decay, w0, hw, hb):
    groups, _, rows, _ = pieces[0].shape
    count = len(pieces)
    width = hb * HEAD_DIM

    def kernel(*refs):
        got = refs[:count]
        qw_ref, kw_ref, *results = refs[count:]
        for o in range(groups):
            for h in range(hb):
                c = head_cols(h)
                q, k, v, g = (
                    jnp.concatenate([r[o, a, :, c] for r in got], axis=0) for a in range(4)
                )
                pair = head_states(
                    q, k, v, g, qw_ref[0, o, :, h : h + 1], kw_ref[0, o, :, h : h + 1]
                )
                for t in range(2):
                    results[o][t, h] = pair[t].astype(results[o].dtype)

    piece = pl.BlockSpec((groups, 4, rows, width), lambda i: (0, 0, 0, i))
    weight = pl.BlockSpec((1, groups, count * rows, hb), lambda i: (w0 // hb + i, 0, 0, 0))
    shape = (2, hw, HEAD_DIM, HEAD_DIM)
    return order.call(
        kernel,
        "states",
        [],
        [*pieces, decay[2], decay[3]],
        [piece] * count + [weight] * 2,
        [jax.ShapeDtypeStruct(shape, kind) for kind in (WIDE, LOW)[:groups]],
        [pl.BlockSpec((2, hb, HEAD_DIM, HEAD_DIM), lambda i: (0, i, 0, 0))] * groups,
        grid=(hw // hb,),
    )


def step(order, table, flags, w0, hw, own, parts, around, keep=None, add=None, reach=None,
         single=False, both=False, selects=0, total=False, final=None, extras=()):
    shape = (2, hw, HEAD_DIM, HEAD_DIM)
    hs = math.gcd(hw, STEP)
    inputs = ([] if own is None else [own]) + list(parts)
    inputs += ([] if around is None else [around]) + list(extras)
    out_shape = []
    if total:
        out_shape.append(jax.ShapeDtypeStruct(shape, WIDE))
    if both:
        out_shape.append(jax.ShapeDtypeStruct(shape, LOW))
    out_shape += [jax.ShapeDtypeStruct(shape[1:], LOW)] * selects
    if reach is not None and final is None:
        out_shape.append(jax.ShapeDtypeStruct(shape, WIDE))
    if final is not None:
        out_shape += [jax.ShapeDtypeStruct(shape, LOW)] * (len(final) // 4)

    def kernel(table_ref, flags_ref, *refs):
        refs = list(refs)
        own_ref = None if own is None else refs.pop(0)
        part_refs = [refs.pop(0) for _ in parts]
        around_ref = None if around is None else refs.pop(0)
        extra_refs = [refs.pop(0) for _ in extras]

        first = w0 + pl.program_id(0) * hs

        for h in range(hs):
            out = list(refs)

            def weight(row):
                return table_ref[row, first + h]

            got = [
                [r[h].astype(WIDE)] * 2 if single else [r[t, h].astype(WIDE) for t in range(2)]
                for r in part_refs
            ]
            if keep is not None:
                sums = []
                for t in range(2):
                    value = weight(keep[t]) * own_ref[t, h]
                    for p, part in enumerate(got):
                        value = value + weight(add[p][t]) * part[t]
                    sums.append(value)
                if total:
                    ref = out.pop(0)
                    for t in range(2):
                        ref[t, h] = sums[t]
                if both:
                    ref = out.pop(0)
                    for t in range(2):
                        ref[t, h] = sums[t].astype(LOW)
                for j in range(selects):
                    ref = out.pop(0)
                    ref[h] = jnp.where(flags_ref[j] != 0, sums[1], sums[0]).astype(LOW)
            if reach is not None:
                sides = []
                for t in range(2):
                    value = None if around_ref is None else around_ref[t, h]
                    for p, part in enumerate(got):
                        term = weight(reach[p][t]) * part[t]
                        value = term if value is None else value + term
                    sides.append(value)
                if final is None:
                    ref = out.pop(0)
                    for t in range(2):
                        ref[t, h] = sides[t]
                else:
                    for i, ref in enumerate(out):
                        for t in range(2):
                            value = sides[t]
                            if extra_refs:
                                a, b = final[4 * i + 2 * t : 4 * i + 2 * t + 2]
                                value = weight(a) * value + weight(b) * extra_refs[i][
                                    t, h
                                ].astype(WIDE)
                            ref[t, h] = value.astype(LOW)

    def block(x):
        if len(x.shape) == 3:
            return pl.BlockSpec((hs, HEAD_DIM, HEAD_DIM), lambda i, *_: (i, 0, 0))
        return pl.BlockSpec((2, hs, HEAD_DIM, HEAD_DIM), lambda i, *_: (0, i, 0, 0))

    return order.call(
        kernel,
        "step",
        [table, flags],
        inputs,
        [block(x) for x in inputs],
        out_shape,
        [block(x) for x in out_shape],
        grid=(hw // hs,),
    )


def grads(order, cols, pieces, group, decay, st, outs, full, w0, hw, hb):
    _, _, rows, _ = pieces[0].shape
    count = len(pieces)
    span = count * rows
    width = hb * HEAD_DIM
    aliased = outs is not None
    cumr, cumc, qw, kw, bias = decay
    n_in = count + 6

    def kernel(cols_ref, *refs):
        got = refs[:count]
        qw_ref, kw_ref, cumc_ref, cumr_ref, bias_ref, st_ref = refs[count:n_in]
        results = refs[n_in + (3 if aliased else 0) :]
        kept, sends = results[:3], results[3:]
        for h in range(hb):
            c = head_cols(h)
            q, k, v, g = (
                jnp.concatenate([r[0, a, :, c] for r in got], axis=0) for a in range(4)
            )
            at = (0, 0, slice(None), slice(h, h + 1))
            outputs = head_grads(
                q, k, v, g, qw_ref[at], kw_ref[at], cumc_ref[at],
                cumr_ref[0, 0, h : h + 1, :], bias_ref[...], st_ref[0, h], st_ref[1, h],
            )
            for a, result in enumerate(outputs):
                kept[a][:, c] = result[:rows]
                for m, send in enumerate(sends):
                    send[a, :, c] = result[(m + 1) * rows : (m + 2) * rows]

    piece = pl.BlockSpec((1, 4, rows, width), lambda i, c: (group, 0, 0, i))
    column = pl.BlockSpec((1, 1, span, hb), lambda i, c: (w0 // hb + i, group, 0, 0))
    row = pl.BlockSpec((1, 1, hb, span), lambda i, c: (w0 // hb + i, group, 0, 0))
    whole = pl.BlockSpec((span, span), lambda i, c: (0, 0))
    state_block = pl.BlockSpec((2, hb, HEAD_DIM, HEAD_DIM), lambda i, c: (0, i, 0, 0))
    results = order.call(
        kernel,
        "grads",
        [cols],
        [*pieces, qw, kw, cumc, cumr, bias, st] + (list(outs) if aliased else []),
        [piece] * count
        + [column] * 3
        + [row, whole, state_block]
        + ([ANY] * 3 if aliased else []),
        [jax.ShapeDtypeStruct((rows, full), LOW)] * 3
        + [jax.ShapeDtypeStruct((3, rows, hw * HEAD_DIM), LOW)] * (count - 1),
        [pl.BlockSpec((rows, width), lambda i, c: (0, c[group] + i))] * 3
        + [pl.BlockSpec((3, rows, width), lambda i, c: (0, 0, i))] * (count - 1),
        grid=(hw // hb,),
        aliases={1 + n_in + a: a for a in range(3)} if aliased else {},
    )
    return (results[:3], results[3:])


def place(order, ats, parts, outs):
    rows, full = outs[0].shape
    count = len(parts)

    def kernel(at_ref, *refs):
        ins, results = refs[:count], refs[count + 3 : count + 6]
        buffers, sems = refs[count + 6 : -1], refs[-1]
        loads, stores = [], []
        for p, ref in enumerate(ins):
            columns = pl.ds(pl.multiple_of(at_ref[p] * HEAD_DIM, HEAD_DIM), ref.shape[2])
            loads.append(pltpu.make_async_copy(ref, buffers[p], sems.at[4 * p + 3]))
            for a in range(3):
                stores.append(
                    pltpu.make_async_copy(
                        buffers[p].at[a], results[a].at[:, columns], sems.at[4 * p + a]
                    )
                )
        for load in loads:
            load.start()
        for p, load in enumerate(loads):
            load.wait()
            for store in stores[3 * p : 3 * p + 3]:
                store.start()
        for store in stores:
            store.wait()

    return order.call(
        kernel,
        "place",
        [jnp.stack(ats)],
        [*parts, *outs],
        [ANY] * (count + 3),
        [jax.ShapeDtypeStruct((rows, full), LOW)] * 3,
        [ANY] * 3,
        scratch=[pltpu.VMEM(p.shape, LOW) for p in parts]
        + [pltpu.SemaphoreType.DMA((4 * count,))],
        aliases={1 + count + a: a for a in range(3)},
    )


class Table:
    def __init__(self, log_decay, low):
        self.peers = lax.axis_size("seq")
        self.me = lax.axis_index("seq")
        sums = jnp.sum(log_decay.reshape(log_decay.shape[0], 2, -1), axis=2)
        self.lo, self.hi, self.on, self.gate = [], [], [], []
        self.sums = sums
        every = (sums[:, 0] + sums[:, 1])[None]
        bit = 1
        while bit < self.peers:
            other = swap(every, "seq", bit)
            late = (self.me & bit) != 0
            every = jnp.where(
                late,
                jnp.concatenate([other, every], axis=0),
                jnp.concatenate([every, other], axis=0),
            )
            bit *= 2
        self.every = jnp.concatenate([every, sums.T], axis=0)

    def row(self, a, b, on=True):
        self.lo.append(jnp.asarray(a, jnp.int32))
        self.hi.append(jnp.asarray(b, jnp.int32))
        self.on.append(jnp.asarray(on, jnp.bool_))
        return len(self.lo) - 1

    def one_if(self, on):
        return self.row(0, 0, on)

    def half_if(self, which, use):
        at = self.peers + which
        return self.row(jnp.where(use, at, 0), jnp.where(use, at + 1, 0))

    def build(self):
        index = jnp.arange(self.peers + 2)[None, :]
        inside = (index >= jnp.stack(self.lo)[:, None]) & (index < jnp.stack(self.hi)[:, None])
        total = jnp.sum(jnp.where(inside[:, :, None], self.every[None], 0.0), axis=1)
        return jnp.where(jnp.stack(self.on)[:, None], jnp.exp(total), 0.0)


def seq_levels(table):
    bits = table.peers.bit_length() - 1
    me = table.me
    levels = []
    base = 0
    while base < bits:
        nb = min(1 if base == 0 else 2, bits - base)
        size = 1 << base
        start = me - me % size
        above = me - me % (size << nb)
        end = above + (size << nb)
        last = base + nb == bits
        level = dict(base=base, nb=nb, last=last, reach=[], add=[], keep=None)
        if not last:
            level["keep"] = (table.row(start + size, end), table.row(above, start))
        for p in range(1, 1 << nb):
            other = start ^ (p << base)
            level["reach"].append(
                (
                    table.row(other + size, me, other < start),
                    table.row(me + 1, other, other > start),
                )
            )
            if not last:
                level["add"].append((table.row(other + size, end), table.row(above, other)))
        levels.append(level)
        base += nb
    return levels


class Wave:
    def __init__(self, env, mode, w0, hw):
        self.env, self.mode, self.w0, self.hw = env, mode, w0, hw
        self.peers = range(1, env.n // 2 if mode == "P" else env.n)
        self.parts = []

    def columns(self, device):
        at = [device, device ^ (self.env.n // 2)] if self.mode == "P" else [device]
        return (jnp.stack(at) * self.env.heads + self.w0).astype(jnp.int32)

    def pack(self):
        e = self.env
        self.received = [None] * len(self.peers)
        for m in sorted(self.peers, reverse=True):
            packed = pack(e.order, self.columns(e.z ^ m), e.arrays, self.hw, e.after)
            self.received[m - 1] = swap(packed, "head", m)

    def keep(self):
        e = self.env
        self.kept = pack(e.order, self.columns(e.z), e.arrays, self.hw, vmem=VMEM)
        self.pieces = [self.kept] + self.received

    def states(self):
        e = self.env
        self.decay = e.decay[self.mode]
        self.level = 0
        self.around = None
        self.own, *send = states(e.order, self.pieces, self.decay, self.w0, self.hw, e.hb)
        if send:
            self.theirs = swap(send[0], "head", e.n // 2)

    def begin(self):
        e = self.env
        levels = e.levels
        if not levels:
            return
        level = levels[0]
        result = step(
            e.order, e.table, e.flags, self.w0, self.hw, self.own,
            [self.theirs] if self.mode == "P" else [], None,
            keep=e.comb[0] if self.mode == "P" else e.ones,
            add=[e.comb[1]] if self.mode == "P" else [],
            total=not level["last"], both=not level["last"],
            selects=level["nb"] if level["last"] else 0,
        )
        self.exchange(result, level)

    def exchange(self, result, level):
        if level["last"]:
            sends = result
        else:
            self.total = result[0]
            sends = [result[1]]
        self.got = []
        for p in range(1, 1 << level["nb"]):
            send = sends[p.bit_length() - 1] if level["last"] else sends[0]
            self.got.append(swap(send, "seq", p << level["base"]))

    def advance(self):
        e = self.env
        level, after = e.levels[self.level], e.levels[self.level + 1]
        result = step(
            e.order, e.table, e.flags, self.w0, self.hw, self.total, self.got, self.around,
            keep=level["keep"], add=level["add"], reach=level["reach"],
            total=not after["last"], both=not after["last"],
            selects=after["nb"] if after["last"] else 0,
        )
        self.around = result.pop()
        self.level += 1
        self.exchange(result, after)

    def finish(self):
        e = self.env
        level = e.levels[-1] if e.levels else None
        zero = jnp.zeros((2, self.hw, HEAD_DIM, HEAD_DIM), WIDE)
        result = step(
            e.order, e.table, e.flags, self.w0, self.hw, None,
            self.got if level else [], self.around if level and len(e.levels) > 1 else zero,
            reach=level["reach"] if level else [], single=True,
            final=e.final if self.mode == "P" else e.ones * 2,
            extras=[self.theirs, self.own] if self.mode == "P" else [],
        )
        self.own_states = result[0]
        if self.mode == "P":
            self.mirror_states = swap(result[1], "head", e.n // 2)

    def touch(self):
        self.env.order.call(lambda *refs: None, "touch", [], [self.mirror_states], [ANY], [], [])

    def grads(self, group):
        e = self.env
        st = self.mirror_states if group else self.own_states
        e.outs, sends = grads(
            e.order, self.columns(e.z) // e.hb, self.pieces, group, self.decay, st, e.outs,
            e.arrays[0].shape[1], self.w0, self.hw, e.hb,
        )
        for m in sorted(self.peers, reverse=True):
            at = self.columns(e.z ^ m)[group]
            self.parts.append((at, swap(sends[m - 1], "head", m)))

    def place(self):
        e = self.env
        if self.parts:
            e.outs = place(
                e.order, [t[0] for t in self.parts], [t[1] for t in self.parts], e.outs
            )
            self.parts = []


class Env:
    pass


def local(queries, key_rows, value_rows, out_grad, log_decay):
    e = Env()
    e.arrays = (queries, key_rows, value_rows, out_grad)
    rows = queries.shape[0]
    e.heads = heads = log_decay.shape[0]
    e.hb = math.gcd(heads, PART)
    e.n = n = lax.axis_size("head")
    e.z = z = lax.axis_index("head")
    e.order = Order()
    e.outs = None
    e.decay = {}
    e.after = ()
    half = n // 2
    low = z < half

    def prepare(modes):
        table = Table(log_decay, low)
        e.levels = seq_levels(table)
        e.ones = (table.one_if(True),) * 2
        e.comb = (
            (table.half_if(1, low), table.half_if(0, ~low)),
            (table.half_if(1, ~low), table.half_if(0, low)),
        )
        off, on = table.one_if(~low), table.one_if(low)
        e.final = (
            table.half_if(0, ~low), off, table.half_if(1, low), on,
            table.half_if(0, low), on, table.half_if(1, ~low), off,
        )
        e.table = table.build()
        e.after = (e.table,)
        top = e.levels[-1] if e.levels else dict(base=0, nb=1)
        e.flags = jnp.stack(
            [(table.me >> (top["base"] + j)) & 1 for j in range(top["nb"])]
        ).astype(jnp.int32)
        if "P" in modes:
            at = jnp.stack([z % half, z // half]).astype(jnp.int32)
            mirror = swap(log_decay, "head", half)
            e.decay["P"] = decays(e.order, at, [log_decay, mirror], rows, half, e.hb)
        if "X" in modes:
            at = jnp.stack([z, z * 0]).astype(jnp.int32)
            e.decay["X"] = decays(e.order, at, [log_decay], rows, n, e.hb)

    schedule(e, heads, prepare)
    return tuple(e.outs)


WAVES = ("P8", "P8")
STEPS = ("pa", "pb", "x", "ka", "sa", "kb", "sb", "ba", "va", "fa", "bb", "vb", "ga", "ta", "fb", "gb", "ha", "hb", "la", "lb")


def schedule(e, heads, prepare):
    sizes, steps = WAVES, STEPS
    if heads % 16:
        sizes, steps = ("P16",), ("pa", "x", "ka", "sa", "ba", "va", "fa", "ga", "ha", "la")
    waves, w0 = {}, 0
    for name, size in zip("abcdef", sizes):
        hw = int(size[1:]) * heads // 16
        waves[name] = Wave(e, size[0], w0, hw)
        w0 += hw
    for code in steps:
        if code == "x":
            prepare({size[0] for size in sizes})
            continue
        wave = waves[code[1]]
        if code[0] == "p":
            wave.pack()
        elif code[0] == "k":
            wave.keep()
        elif code[0] == "s":
            wave.states()
        elif code[0] == "b":
            wave.begin()
        elif code[0] == "v":
            for _ in e.levels[1:]:
                wave.advance()
        elif code[0] == "f":
            wave.finish()
        elif code[0] == "g":
            wave.grads(0)
        elif code[0] == "h":
            wave.grads(1)
        elif code[0] == "l":
            wave.place()
        elif code[0] == "t":
            wave.touch()


def solution(mesh):
    rows = P(("seq", "head"), None)
    return jax.shard_map(
        local,
        mesh=mesh,
        in_specs=(rows, rows, rows, rows, P("head", "seq")),
        out_specs=(rows, rows, rows),
        check_vma=False,
    )
```

```python
import functools
import math

import jax
import jax.numpy as jnp
from jax import lax
from jax.experimental import pallas as pl
from jax.experimental.pallas import tpu as pltpu
from jax.sharding import PartitionSpec as P

HEAD_DIM = 128
PART = 4
STEP = 8
VMEM = 16 * 1024 * 1024
ANY = pl.BlockSpec(memory_space=pl.ANY)
FULL = pl.BlockSpec(memory_space=pltpu.VMEM)
SCALARS = pl.BlockSpec(memory_space=pltpu.SMEM)
NN = ((1,), (0,))
NT = ((1,), (1,))
TN = ((0,), (0,))
LOW = jnp.bfloat16
COST = pl.CostEstimate(flops=1, bytes_accessed=1, transcendentals=0)
GRADS_COST = pl.CostEstimate(flops=4000000000, bytes_accessed=1, transcendentals=0)
WIDE = jnp.float32


def swap(x, axis, bit):
    return lax.ppermute(x, axis, [(i, i ^ bit) for i in range(lax.axis_size(axis))])


def dot(a, b, dims):
    return lax.dot_general(a, b, (dims, ((), ())), preferred_element_type=WIDE)


def head_cols(h):
    return slice(h * HEAD_DIM, (h + 1) * HEAD_DIM)


class Order:
    def __init__(self):
        self.token = None

    def call(
        self,
        kernel,
        name,
        scalars,
        inputs,
        in_specs,
        out_shape,
        out_specs,
        grid=(),
        scratch=(),
        aliases=None,
        after=(),
        vmem=VMEM,
    ):
        extra = list(after) + ([] if self.token is None else [self.token])
        n_scalars, n_in, n_out = len(scalars), len(inputs), len(out_shape)

        def body(*refs):
            first = n_scalars + n_in
            second = first + len(extra)
            kernel(*refs[:first], *refs[second : second + n_out], *refs[second + n_out + 1 :])

        *results, self.token = pl.pallas_call(
            body,
            grid_spec=pltpu.PrefetchScalarGridSpec(
                num_scalar_prefetch=n_scalars,
                grid=grid,
                in_specs=list(in_specs) + [ANY] * len(extra),
                out_specs=list(out_specs) + [ANY],
                scratch_shapes=scratch,
            ),
            out_shape=list(out_shape) + [jax.ShapeDtypeStruct((8, 128), WIDE)],
            input_output_aliases=aliases or {},
            compiler_params=pltpu.CompilerParams(vmem_limit_bytes=vmem),
            cost_estimate=GRADS_COST if name == "grads" else COST,
            name=name,
        )(*scalars, *inputs, *extra)
        return results


def head_states(q, k, v, g, qw, kw):
    ks = (k.astype(WIDE) * kw).astype(LOW)
    qs = (q.astype(WIDE) * qw).astype(LOW)
    return dot(ks, v, TN), dot(qs, g, TN)


def head_grads(q, k, v, g, qw, kw, cumc, cumr, bias, forward, backward):
    decay = jnp.exp(cumc - cumr + bias)
    gs = (dot(g, v, NT) * decay).astype(LOW)
    sc = (dot(q, k, NT) * decay).astype(LOW)
    dq = dot(gs, k, NN) + qw * dot(g, forward, NT)
    dk = dot(gs, q, TN) + kw * dot(v, backward, NT)
    dv = dot(sc, g, TN) + kw * dot(k, backward, NN)
    return dq.astype(LOW), dk.astype(LOW), dv.astype(LOW)


def pack(order, target, arrays, hw, after=(), vmem=60 * 1024 * 1024):
    rows = arrays[0].shape[0]
    width = hw * HEAD_DIM
    groups = target.shape[0]

    def kernel(at_ref, *refs):
        ins, out, sems = refs[:4], refs[4], refs[5]
        copies = []
        for o in range(groups):
            columns = pl.ds(pl.multiple_of(at_ref[o] * HEAD_DIM, HEAD_DIM), width)
            for a, ref in enumerate(ins):
                copies.append(
                    pltpu.make_async_copy(
                        ref.at[:, columns], out.at[o, a], sems.at[len(copies)]
                    )
                )
        for copy in copies:
            copy.start()
        for copy in copies:
            copy.wait()

    (packed,) = order.call(
        kernel,
        "pack",
        [target],
        arrays,
        [pl.BlockSpec(memory_space=pltpu.HBM)] * 4,
        [jax.ShapeDtypeStruct((groups, 4, rows, width), LOW)],
        [FULL],
        scratch=[pltpu.SemaphoreType.DMA((4 * groups,))],
        after=after,
        vmem=vmem,
    )
    return packed


def decays(order, at, logs, rows, pieces, hb):
    heads, length = logs[0].shape
    span = pieces * rows
    groups = len(logs)
    steps = heads // hb

    def kernel(at_ref, *refs):
        sources = refs[:groups]
        cumr, cumc, qw, kw, bias = refs[groups:]
        slot, upper = at_ref[0], at_ref[1]

        def position(axis):
            p = lax.broadcasted_iota(jnp.int32, (span, span), axis)
            return ((p // rows) ^ slot) * rows + p % rows

        down, along = position(0), position(1)
        bias[...] = jnp.where(down >= along, 0.0, -1e30)
        source = lax.broadcasted_iota(jnp.int32, (span, span), 0)
        upto = (source <= along).astype(WIDE)
        ones = jnp.ones((span, span), WIDE)
        for o, ref in enumerate(sources):
            rows_in = ref[...]
            if span < length:
                rows_in = jnp.where(upper == 0, rows_in[:, :span], rows_in[:, span:])

            def exact(a, b, dims):
                return lax.dot_general(
                    a,
                    b,
                    (dims, ((), ())),
                    precision=lax.Precision.HIGHEST,
                    preferred_element_type=WIDE,
                )

            line = exact(rows_in, upto, NN)
            column = exact(upto, rows_in, ((0,), (1,)))
            total = exact(ones, rows_in, NT)
            query = jnp.exp(column)
            key = jnp.exp(total - column)
            for i in range(steps):
                part = slice(i * hb, (i + 1) * hb)
                cumr[i, o] = line[part]
                cumc[i, o] = column[:, part]
                qw[i, o] = query[:, part]
                kw[i, o] = key[:, part]

    columns = jax.ShapeDtypeStruct((steps, groups, span, hb), WIDE)
    return order.call(
        kernel,
        "decays",
        [at],
        logs,
        [FULL] * groups,
        [
            jax.ShapeDtypeStruct((steps, groups, hb, span), WIDE),
            columns,
            columns,
            columns,
            jax.ShapeDtypeStruct((span, span), WIDE),
        ],
        [FULL] * 5,
    )


def states(order, pieces, decay, w0, hw, hb):
    groups, _, rows, _ = pieces[0].shape
    count = len(pieces)
    width = hb * HEAD_DIM

    def kernel(*refs):
        got = refs[:count]
        qw_ref, kw_ref, *results = refs[count:]
        for o in range(groups):
            for h in range(hb):
                c = head_cols(h)
                q, k, v, g = (
                    jnp.concatenate([r[o, a, :, c] for r in got], axis=0) for a in range(4)
                )
                pair = head_states(
                    q, k, v, g, qw_ref[0, o, :, h : h + 1], kw_ref[0, o, :, h : h + 1]
                )
                for t in range(2):
                    results[o][t, h] = pair[t].astype(results[o].dtype)

    piece = pl.BlockSpec((groups, 4, rows, width), lambda i: (0, 0, 0, i))
    weight = pl.BlockSpec((1, groups, count * rows, hb), lambda i: (w0 // hb + i, 0, 0, 0))
    shape = (2, hw, HEAD_DIM, HEAD_DIM)
    return order.call(
        kernel,
        "states",
        [],
        [*pieces, decay[2], decay[3]],
        [piece] * count + [weight] * 2,
        [jax.ShapeDtypeStruct(shape, kind) for kind in (WIDE, LOW)[:groups]],
        [pl.BlockSpec((2, hb, HEAD_DIM, HEAD_DIM), lambda i: (0, i, 0, 0))] * groups,
        grid=(hw // hb,),
    )


def step(order, table, flags, w0, hw, own, parts, around, keep=None, add=None, reach=None,
         single=False, both=False, selects=0, total=False, final=None, extras=()):
    shape = (2, hw, HEAD_DIM, HEAD_DIM)
    hs = math.gcd(hw, STEP)
    inputs = ([] if own is None else [own]) + list(parts)
    inputs += ([] if around is None else [around]) + list(extras)
    out_shape = []
    if total:
        out_shape.append(jax.ShapeDtypeStruct(shape, WIDE))
    if both:
        out_shape.append(jax.ShapeDtypeStruct(shape, LOW))
    out_shape += [jax.ShapeDtypeStruct(shape[1:], LOW)] * selects
    if reach is not None and final is None:
        out_shape.append(jax.ShapeDtypeStruct(shape, WIDE))
    if final is not None:
        out_shape += [jax.ShapeDtypeStruct(shape, LOW)] * (len(final) // 4)

    def kernel(table_ref, flags_ref, *refs):
        refs = list(refs)
        own_ref = None if own is None else refs.pop(0)
        part_refs = [refs.pop(0) for _ in parts]
        around_ref = None if around is None else refs.pop(0)
        extra_refs = [refs.pop(0) for _ in extras]

        first = w0 + pl.program_id(0) * hs

        for h in range(hs):
            out = list(refs)

            def weight(row):
                return table_ref[row, first + h]

            got = [
                [r[h].astype(WIDE)] * 2 if single else [r[t, h].astype(WIDE) for t in range(2)]
                for r in part_refs
            ]
            if keep is not None:
                sums = []
                for t in range(2):
                    value = weight(keep[t]) * own_ref[t, h]
                    for p, part in enumerate(got):
                        value = value + weight(add[p][t]) * part[t]
                    sums.append(value)
                if total:
                    ref = out.pop(0)
                    for t in range(2):
                        ref[t, h] = sums[t]
                if both:
                    ref = out.pop(0)
                    for t in range(2):
                        ref[t, h] = sums[t].astype(LOW)
                for j in range(selects):
                    ref = out.pop(0)
                    ref[h] = jnp.where(flags_ref[j] != 0, sums[1], sums[0]).astype(LOW)
            if reach is not None:
                sides = []
                for t in range(2):
                    value = None if around_ref is None else around_ref[t, h]
                    for p, part in enumerate(got):
                        term = weight(reach[p][t]) * part[t]
                        value = term if value is None else value + term
                    sides.append(value)
                if final is None:
                    ref = out.pop(0)
                    for t in range(2):
                        ref[t, h] = sides[t]
                else:
                    for i, ref in enumerate(out):
                        for t in range(2):
                            value = sides[t]
                            if extra_refs:
                                a, b = final[4 * i + 2 * t : 4 * i + 2 * t + 2]
                                value = weight(a) * value + weight(b) * extra_refs[i][
                                    t, h
                                ].astype(WIDE)
                            ref[t, h] = value.astype(LOW)

    def block(x):
        if len(x.shape) == 3:
            return pl.BlockSpec((hs, HEAD_DIM, HEAD_DIM), lambda i, *_: (i, 0, 0))
        return pl.BlockSpec((2, hs, HEAD_DIM, HEAD_DIM), lambda i, *_: (0, i, 0, 0))

    return order.call(
        kernel,
        "step",
        [table, flags],
        inputs,
        [block(x) for x in inputs],
        out_shape,
        [block(x) for x in out_shape],
        grid=(hw // hs,),
    )


def grads(order, cols, pieces, group, decay, st, outs, full, w0, hw, hb):
    _, _, rows, _ = pieces[0].shape
    count = len(pieces)
    span = count * rows
    width = hb * HEAD_DIM
    aliased = outs is not None
    cumr, cumc, qw, kw, bias = decay
    n_in = count + 6

    def kernel(cols_ref, *refs):
        got = refs[:count]
        qw_ref, kw_ref, cumc_ref, cumr_ref, bias_ref, st_ref = refs[count:n_in]
        results = refs[n_in + (3 if aliased else 0) :]
        kept, sends = results[:3], results[3:]
        for h in range(hb):
            c = head_cols(h)
            q, k, v, g = (
                jnp.concatenate([r[0, a, :, c] for r in got], axis=0) for a in range(4)
            )
            at = (0, 0, slice(None), slice(h, h + 1))
            outputs = head_grads(
                q, k, v, g, qw_ref[at], kw_ref[at], cumc_ref[at],
                cumr_ref[0, 0, h : h + 1, :], bias_ref[...], st_ref[0, h], st_ref[1, h],
            )
            for a, result in enumerate(outputs):
                kept[a][:, c] = result[:rows]
                for m, send in enumerate(sends):
                    send[a, :, c] = result[(m + 1) * rows : (m + 2) * rows]

    piece = pl.BlockSpec((1, 4, rows, width), lambda i, c: (group, 0, 0, i))
    column = pl.BlockSpec((1, 1, span, hb), lambda i, c: (w0 // hb + i, group, 0, 0))
    row = pl.BlockSpec((1, 1, hb, span), lambda i, c: (w0 // hb + i, group, 0, 0))
    whole = pl.BlockSpec((span, span), lambda i, c: (0, 0))
    state_block = pl.BlockSpec((2, hb, HEAD_DIM, HEAD_DIM), lambda i, c: (0, i, 0, 0))
    results = order.call(
        kernel,
        "grads",
        [cols],
        [*pieces, qw, kw, cumc, cumr, bias, st] + (list(outs) if aliased else []),
        [piece] * count
        + [column] * 3
        + [row, whole, state_block]
        + ([ANY] * 3 if aliased else []),
        [jax.ShapeDtypeStruct((rows, full), LOW)] * 3
        + [jax.ShapeDtypeStruct((3, rows, hw * HEAD_DIM), LOW)] * (count - 1),
        [pl.BlockSpec((rows, width), lambda i, c: (0, c[group] + i))] * 3
        + [pl.BlockSpec((3, rows, width), lambda i, c: (0, 0, i))] * (count - 1),
        grid=(hw // hb,),
        aliases={1 + n_in + a: a for a in range(3)} if aliased else {},
    )
    return (results[:3], results[3:])


def place(order, ats, parts, outs):
    rows, full = outs[0].shape
    count = len(parts)

    def kernel(at_ref, *refs):
        ins, results, sems = refs[:count], refs[count + 3 : count + 6], refs[count + 6]
        copies = []
        for p, ref in enumerate(ins):
            columns = pl.ds(pl.multiple_of(at_ref[p] * HEAD_DIM, HEAD_DIM), ref.shape[2])
            for a in range(3):
                copies.append(
                    pltpu.make_async_copy(
                        ref.at[a], results[a].at[:, columns], sems.at[len(copies)]
                    )
                )
        for copy in copies:
            copy.start()
        for copy in copies:
            copy.wait()

    return order.call(
        kernel,
        "place",
        [jnp.stack(ats)],
        [*parts, *outs],
        [FULL] * count + [ANY] * 3,
        [jax.ShapeDtypeStruct((rows, full), LOW)] * 3,
        [ANY] * 3,
        scratch=[pltpu.SemaphoreType.DMA((3 * count,))],
        aliases={1 + count + a: a for a in range(3)},
    )


class Table:
    def __init__(self, log_decay, low):
        self.peers = lax.axis_size("seq")
        self.me = lax.axis_index("seq")
        sums = jnp.sum(log_decay.reshape(log_decay.shape[0], 2, -1), axis=2)
        self.lo, self.hi, self.on, self.gate = [], [], [], []
        self.sums = sums
        every = (sums[:, 0] + sums[:, 1])[None]
        bit = 1
        while bit < self.peers:
            other = swap(every, "seq", bit)
            late = (self.me & bit) != 0
            every = jnp.where(
                late,
                jnp.concatenate([other, every], axis=0),
                jnp.concatenate([every, other], axis=0),
            )
            bit *= 2
        self.every = jnp.concatenate([every, sums.T], axis=0)

    def row(self, a, b, on=True):
        self.lo.append(jnp.asarray(a, jnp.int32))
        self.hi.append(jnp.asarray(b, jnp.int32))
        self.on.append(jnp.asarray(on, jnp.bool_))
        return len(self.lo) - 1

    def one_if(self, on):
        return self.row(0, 0, on)

    def half_if(self, which, use):
        at = self.peers + which
        return self.row(jnp.where(use, at, 0), jnp.where(use, at + 1, 0))

    def build(self):
        index = jnp.arange(self.peers + 2)[None, :]
        inside = (index >= jnp.stack(self.lo)[:, None]) & (index < jnp.stack(self.hi)[:, None])
        total = jnp.sum(jnp.where(inside[:, :, None], self.every[None], 0.0), axis=1)
        return jnp.where(jnp.stack(self.on)[:, None], jnp.exp(total), 0.0)


def seq_levels(table):
    bits = table.peers.bit_length() - 1
    me = table.me
    levels = []
    base = 0
    while base < bits:
        nb = min(1 if base == 0 else 2, bits - base)
        size = 1 << base
        start = me - me % size
        above = me - me % (size << nb)
        end = above + (size << nb)
        last = base + nb == bits
        level = dict(base=base, nb=nb, last=last, reach=[], add=[], keep=None)
        if not last:
            level["keep"] = (table.row(start + size, end), table.row(above, start))
        for p in range(1, 1 << nb):
            other = start ^ (p << base)
            level["reach"].append(
                (
                    table.row(other + size, me, other < start),
                    table.row(me + 1, other, other > start),
                )
            )
            if not last:
                level["add"].append((table.row(other + size, end), table.row(above, other)))
        levels.append(level)
        base += nb
    return levels


class Wave:
    def __init__(self, env, mode, w0, hw):
        self.env, self.mode, self.w0, self.hw = env, mode, w0, hw
        self.peers = range(1, env.n // 2 if mode == "P" else env.n)
        self.parts = []

    def columns(self, device):
        at = [device, device ^ (self.env.n // 2)] if self.mode == "P" else [device]
        return (jnp.stack(at) * self.env.heads + self.w0).astype(jnp.int32)

    def pack(self):
        e = self.env
        self.received = [None] * len(self.peers)
        for m in sorted(self.peers, reverse=True):
            packed = pack(e.order, self.columns(e.z ^ m), e.arrays, self.hw, e.after)
            self.received[m - 1] = swap(packed, "head", m)

    def keep(self):
        e = self.env
        self.kept = pack(e.order, self.columns(e.z), e.arrays, self.hw, vmem=VMEM)
        self.pieces = [self.kept] + self.received

    def states(self):
        e = self.env
        self.decay = e.decay[self.mode]
        self.level = 0
        self.around = None
        self.own, *send = states(e.order, self.pieces, self.decay, self.w0, self.hw, e.hb)
        if send:
            self.theirs = swap(send[0], "head", e.n // 2)

    def begin(self):
        e = self.env
        levels = e.levels
        if not levels:
            return
        level = levels[0]
        result = step(
            e.order, e.table, e.flags, self.w0, self.hw, self.own,
            [self.theirs] if self.mode == "P" else [], None,
            keep=e.comb[0] if self.mode == "P" else e.ones,
            add=[e.comb[1]] if self.mode == "P" else [],
            total=not level["last"], both=not level["last"],
            selects=level["nb"] if level["last"] else 0,
        )
        self.exchange(result, level)

    def exchange(self, result, level):
        if level["last"]:
            sends = result
        else:
            self.total = result[0]
            sends = [result[1]]
        self.got = []
        for p in range(1, 1 << level["nb"]):
            send = sends[p.bit_length() - 1] if level["last"] else sends[0]
            self.got.append(swap(send, "seq", p << level["base"]))

    def advance(self):
        e = self.env
        level, after = e.levels[self.level], e.levels[self.level + 1]
        result = step(
            e.order, e.table, e.flags, self.w0, self.hw, self.total, self.got, self.around,
            keep=level["keep"], add=level["add"], reach=level["reach"],
            total=not after["last"], both=not after["last"],
            selects=after["nb"] if after["last"] else 0,
        )
        self.around = result.pop()
        self.level += 1
        self.exchange(result, after)

    def finish(self):
        e = self.env
        level = e.levels[-1] if e.levels else None
        zero = jnp.zeros((2, self.hw, HEAD_DIM, HEAD_DIM), WIDE)
        result = step(
            e.order, e.table, e.flags, self.w0, self.hw, None,
            self.got if level else [], self.around if level and len(e.levels) > 1 else zero,
            reach=level["reach"] if level else [], single=True,
            final=e.final if self.mode == "P" else e.ones * 2,
            extras=[self.theirs, self.own] if self.mode == "P" else [],
        )
        self.own_states = result[0]
        if self.mode == "P":
            self.mirror_states = swap(result[1], "head", e.n // 2)

    def touch(self):
        self.env.order.call(lambda *refs: None, "touch", [], [self.mirror_states], [ANY], [], [])

    def arrive(self):
        e = self.env
        count = len(self.received)
        e.order.call(lambda *refs: None, "arrive", [], self.received, [ANY] * count, [], [])

    def grads(self, group):
        e = self.env
        st = self.mirror_states if group else self.own_states
        e.outs, sends = grads(
            e.order, self.columns(e.z) // e.hb, self.pieces, group, self.decay, st, e.outs,
            e.arrays[0].shape[1], self.w0, self.hw, e.hb,
        )
        for m in sorted(self.peers, reverse=True):
            at = self.columns(e.z ^ m)[group]
            self.parts.append((at, swap(sends[m - 1], "head", m)))

    def place(self):
        e = self.env
        if self.parts:
            e.outs = place(
                e.order, [t[0] for t in self.parts], [t[1] for t in self.parts], e.outs
            )
            self.parts = []


class Env:
    pass


def local(queries, key_rows, value_rows, out_grad, log_decay):
    e = Env()
    e.arrays = (queries, key_rows, value_rows, out_grad)
    rows = queries.shape[0]
    e.heads = heads = log_decay.shape[0]
    e.hb = math.gcd(heads, PART)
    e.n = n = lax.axis_size("head")
    e.z = z = lax.axis_index("head")
    e.order = Order()
    e.outs = None
    e.decay = {}
    e.after = ()
    half = n // 2
    low = z < half

    def prepare(modes):
        table = Table(log_decay, low)
        e.levels = seq_levels(table)
        e.ones = (table.one_if(True),) * 2
        e.comb = (
            (table.half_if(1, low), table.half_if(0, ~low)),
            (table.half_if(1, ~low), table.half_if(0, low)),
        )
        off, on = table.one_if(~low), table.one_if(low)
        e.final = (
            table.half_if(0, ~low), off, table.half_if(1, low), on,
            table.half_if(0, low), on, table.half_if(1, ~low), off,
        )
        e.table = table.build()
        e.after = (e.table,)
        top = e.levels[-1] if e.levels else dict(base=0, nb=1)
        e.flags = jnp.stack(
            [(table.me >> (top["base"] + j)) & 1 for j in range(top["nb"])]
        ).astype(jnp.int32)
        if "P" in modes:
            at = jnp.stack([z % half, z // half]).astype(jnp.int32)
            mirror = swap(log_decay, "head", half)
            e.decay["P"] = decays(e.order, at, [log_decay, mirror], rows, half, e.hb)
        if "X" in modes:
            at = jnp.stack([z, z * 0]).astype(jnp.int32)
            e.decay["X"] = decays(e.order, at, [log_decay], rows, n, e.hb)

    schedule(e, heads, prepare)
    return tuple(e.outs)


WAVES = ("P8", "P8")
STEPS = ("pa", "pb", "ua", "x", "ka", "kb", "sa", "sb", "ba", "va", "fa", "bb", "vb", "ga", "ta", "fb", "gb", "la", "ha", "hb", "la", "lb")


def schedule(e, heads, prepare):
    sizes, steps = WAVES, STEPS
    if heads % 16:
        sizes, steps = ("P16",), ("pa", "x", "ka", "sa", "ba", "va", "fa", "ga", "ha", "la")
    waves, w0 = {}, 0
    for name, size in zip("abcdef", sizes):
        hw = int(size[1:]) * heads // 16
        waves[name] = Wave(e, size[0], w0, hw)
        w0 += hw
    for code in steps:
        if code == "x":
            prepare({size[0] for size in sizes})
            continue
        wave = waves[code[1]]
        if code[0] == "p":
            wave.pack()
        elif code[0] == "k":
            wave.keep()
        elif code[0] == "s":
            wave.states()
        elif code[0] == "b":
            wave.begin()
        elif code[0] == "v":
            for _ in e.levels[1:]:
                wave.advance()
        elif code[0] == "f":
            wave.finish()
        elif code[0] == "g":
            wave.grads(0)
        elif code[0] == "h":
            wave.grads(1)
        elif code[0] == "l":
            wave.place()
        elif code[0] == "t":
            wave.touch()
        elif code[0] == "u":
            wave.arrive()


def solution(mesh):
    rows = P(("seq", "head"), None)
    return jax.shard_map(
        local,
        mesh=mesh,
        in_specs=(rows, rows, rows, rows, P("head", "seq")),
        out_specs=(rows, rows, rows),
        check_vma=False,
    )
```

```python
import functools
import math

import jax
import jax.numpy as jnp
from jax import lax
from jax.experimental import pallas as pl
from jax.experimental.pallas import tpu as pltpu
from jax.sharding import PartitionSpec as P

HEAD_DIM = 128
PART = 4
STEP = 8
VMEM = 16 * 1024 * 1024
ANY = pl.BlockSpec(memory_space=pl.ANY)
FULL = pl.BlockSpec(memory_space=pltpu.VMEM)
SCALARS = pl.BlockSpec(memory_space=pltpu.SMEM)
NN = ((1,), (0,))
NT = ((1,), (1,))
TN = ((0,), (0,))
LOW = jnp.bfloat16
COST = pl.CostEstimate(flops=1, bytes_accessed=1, transcendentals=0)
TOUCH_COST = pl.CostEstimate(flops=1, bytes_accessed=1, transcendentals=0)
GRADS_COST = pl.CostEstimate(flops=4000000000, bytes_accessed=1, transcendentals=0)
WIDE = jnp.float32


def swap(x, axis, bit):
    return lax.ppermute(x, axis, [(i, i ^ bit) for i in range(lax.axis_size(axis))])


def dot(a, b, dims):
    return lax.dot_general(a, b, (dims, ((), ())), preferred_element_type=WIDE)


def head_cols(h):
    return slice(h * HEAD_DIM, (h + 1) * HEAD_DIM)


class Order:
    def __init__(self):
        self.token = None

    def call(
        self,
        kernel,
        name,
        scalars,
        inputs,
        in_specs,
        out_shape,
        out_specs,
        grid=(),
        scratch=(),
        aliases=None,
        after=(),
        vmem=VMEM,
    ):
        extra = list(after) + ([] if self.token is None else [self.token])
        n_scalars, n_in, n_out = len(scalars), len(inputs), len(out_shape)

        def body(*refs):
            first = n_scalars + n_in
            second = first + len(extra)
            kernel(*refs[:first], *refs[second : second + n_out], *refs[second + n_out + 1 :])

        *results, self.token = pl.pallas_call(
            body,
            grid_spec=pltpu.PrefetchScalarGridSpec(
                num_scalar_prefetch=n_scalars,
                grid=grid,
                in_specs=list(in_specs) + [ANY] * len(extra),
                out_specs=list(out_specs) + [ANY],
                scratch_shapes=scratch,
            ),
            out_shape=list(out_shape) + [jax.ShapeDtypeStruct((8, 128), WIDE)],
            input_output_aliases=aliases or {},
            compiler_params=pltpu.CompilerParams(vmem_limit_bytes=vmem),
            cost_estimate={"grads": GRADS_COST, "touch": TOUCH_COST}.get(name, COST),
            name=name,
        )(*scalars, *inputs, *extra)
        return results


def head_states(q, k, v, g, qw, kw):
    ks = (k.astype(WIDE) * kw).astype(LOW)
    qs = (q.astype(WIDE) * qw).astype(LOW)
    return dot(ks, v, TN), dot(qs, g, TN)


def head_grads(q, k, v, g, qw, kw, cumc, cumr, bias, forward, backward):
    decay = jnp.exp(cumc - cumr + bias)
    gs = (dot(g, v, NT) * decay).astype(LOW)
    sc = (dot(q, k, NT) * decay).astype(LOW)
    dq = dot(gs, k, NN) + qw * dot(g, forward, NT)
    dk = dot(gs, q, TN) + kw * dot(v, backward, NT)
    dv = dot(sc, g, TN) + kw * dot(k, backward, NN)
    return dq.astype(LOW), dk.astype(LOW), dv.astype(LOW)


def pack(order, target, arrays, hw):
    rows = arrays[0].shape[0]
    width = hw * HEAD_DIM
    groups = target.shape[0]

    def kernel(at_ref, *refs):
        ins, out, sems = refs[:4], refs[4], refs[5]
        copies = []
        for o in range(groups):
            columns = pl.ds(pl.multiple_of(at_ref[o] * HEAD_DIM, HEAD_DIM), width)
            for a, ref in enumerate(ins):
                copies.append(
                    pltpu.make_async_copy(
                        ref.at[:, columns], out.at[o, a], sems.at[len(copies)]
                    )
                )
        for copy in copies:
            copy.start()
        for copy in copies:
            copy.wait()

    (packed,) = order.call(
        kernel,
        "pack",
        [target],
        arrays,
        [pl.BlockSpec(memory_space=pltpu.HBM)] * 4,
        [jax.ShapeDtypeStruct((groups, 4, rows, width), LOW)],
        [FULL],
        scratch=[pltpu.SemaphoreType.DMA((4 * groups,))],
    )
    return packed


def pack_away(order, target, arrays, hw):
    rows = arrays[0].shape[0]
    width = hw * HEAD_DIM
    groups = target.shape[0]
    shape = (groups, 4, rows, width)

    def kernel(at_ref, *refs):
        ins, out, buffer, sems = refs[:4], refs[4], refs[5], refs[6]
        loads, stores = [], []
        for o in range(groups):
            columns = pl.ds(pl.multiple_of(at_ref[o] * HEAD_DIM, HEAD_DIM), width)
            for a, ref in enumerate(ins):
                n = len(loads)
                loads.append(
                    pltpu.make_async_copy(ref.at[:, columns], buffer.at[o, a], sems.at[0, n])
                )
                stores.append(
                    pltpu.make_async_copy(buffer.at[o, a], out.at[o, a], sems.at[1, n])
                )
        for load in loads:
            load.start()
        for load, store in zip(loads, stores):
            load.wait()
            store.start()
        for store in stores:
            store.wait()

    (packed,) = order.call(
        kernel,
        "pack",
        [target],
        arrays,
        [ANY] * 4,
        [jax.ShapeDtypeStruct(shape, LOW)],
        [ANY],
        scratch=[pltpu.VMEM(shape, LOW), pltpu.SemaphoreType.DMA((2, 4 * groups))],
        vmem=60 * 1024 * 1024,
    )
    return packed


def decays(order, at, logs, rows, pieces, hb):
    heads, length = logs[0].shape
    span = pieces * rows
    groups = len(logs)
    steps = heads // hb

    def kernel(at_ref, *refs):
        sources = refs[:groups]
        cumr, cols, bias = refs[groups:]
        slot, upper = at_ref[0], at_ref[1]

        def position(axis):
            p = lax.broadcasted_iota(jnp.int32, (span, span), axis)
            return ((p // rows) ^ slot) * rows + p % rows

        down, along = position(0), position(1)
        bias[...] = jnp.where(down >= along, 0.0, -1e30)
        source = lax.broadcasted_iota(jnp.int32, (span, span), 0)
        upto = (source <= along).astype(WIDE)
        ones = jnp.ones((span, span), WIDE)
        for o, ref in enumerate(sources):
            rows_in = ref[...]
            if span < length:
                rows_in = jnp.where(upper == 0, rows_in[:, :span], rows_in[:, span:])

            def exact(a, b, dims):
                return lax.dot_general(
                    a,
                    b,
                    (dims, ((), ())),
                    precision=lax.Precision.HIGHEST,
                    preferred_element_type=WIDE,
                )

            line = exact(rows_in, upto, NN)
            column = exact(upto, rows_in, ((0,), (1,)))
            total = exact(ones, rows_in, NT)
            query = jnp.exp(column)
            key = jnp.exp(total - column)
            for i in range(steps):
                part = slice(i * hb, (i + 1) * hb)
                cumr[i, o] = line[part]
                for j, value in enumerate((column, query, key)):
                    cols[i, o, :, j * hb : (j + 1) * hb] = value[:, part]

    columns = jax.ShapeDtypeStruct((steps, groups, span, 3 * hb), WIDE)
    return order.call(
        kernel,
        "decays",
        [at],
        logs,
        [FULL] * groups,
        [
            jax.ShapeDtypeStruct((steps, groups, hb, span), WIDE),
            columns,
            jax.ShapeDtypeStruct((span, span), WIDE),
        ],
        [FULL] * 3,
    )


def states(order, pieces, decay, w0, hw, hb):
    groups, _, rows, _ = pieces[0].shape
    count = len(pieces)
    width = hb * HEAD_DIM

    def kernel(*refs):
        got = refs[:count]
        cols_ref, *results = refs[count:]
        for o in range(groups):
            for h in range(hb):
                c = head_cols(h)
                q, k, v, g = (
                    jnp.concatenate([r[o, a, :, c] for r in got], axis=0) for a in range(4)
                )
                qw = cols_ref[0, o, :, hb + h : hb + h + 1]
                kw = cols_ref[0, o, :, 2 * hb + h : 2 * hb + h + 1]
                pair = head_states(q, k, v, g, qw, kw)
                for t in range(2):
                    results[o][t, h] = pair[t].astype(results[o].dtype)

    piece = pl.BlockSpec((groups, 4, rows, width), lambda i: (0, 0, 0, i))
    weight = pl.BlockSpec((1, groups, count * rows, 3 * hb), lambda i: (w0 // hb + i, 0, 0, 0))
    shape = (2, hw, HEAD_DIM, HEAD_DIM)
    return order.call(
        kernel,
        "states",
        [],
        [*pieces, decay[1]],
        [piece] * count + [weight],
        [jax.ShapeDtypeStruct(shape, kind) for kind in (WIDE, LOW)[:groups]],
        [pl.BlockSpec((2, hb, HEAD_DIM, HEAD_DIM), lambda i: (0, i, 0, 0))] * groups,
        grid=(hw // hb,),
    )


def step(order, table, flags, w0, hw, own, parts, around, keep=None, add=None, reach=None,
         single=False, both=False, selects=0, total=False, final=None, extras=()):
    shape = (2, hw, HEAD_DIM, HEAD_DIM)
    hs = math.gcd(hw, STEP)
    inputs = ([] if own is None else [own]) + list(parts)
    inputs += ([] if around is None else [around]) + list(extras)
    out_shape = []
    if total:
        out_shape.append(jax.ShapeDtypeStruct(shape, WIDE))
    if both:
        out_shape.append(jax.ShapeDtypeStruct(shape, LOW))
    out_shape += [jax.ShapeDtypeStruct(shape[1:], LOW)] * selects
    if reach is not None and final is None:
        out_shape.append(jax.ShapeDtypeStruct(shape, WIDE))
    if final is not None:
        out_shape += [jax.ShapeDtypeStruct(shape, LOW)] * (len(final) // 4)

    def kernel(table_ref, flags_ref, *refs):
        refs = list(refs)
        own_ref = None if own is None else refs.pop(0)
        part_refs = [refs.pop(0) for _ in parts]
        around_ref = None if around is None else refs.pop(0)
        extra_refs = [refs.pop(0) for _ in extras]

        first = w0 + pl.program_id(0) * hs

        for h in range(hs):
            out = list(refs)

            def weight(row):
                return table_ref[row, first + h]

            got = [
                [r[h].astype(WIDE)] * 2 if single else [r[t, h].astype(WIDE) for t in range(2)]
                for r in part_refs
            ]
            if keep is not None:
                sums = []
                for t in range(2):
                    value = weight(keep[t]) * own_ref[t, h]
                    for p, part in enumerate(got):
                        value = value + weight(add[p][t]) * part[t]
                    sums.append(value)
                if total:
                    ref = out.pop(0)
                    for t in range(2):
                        ref[t, h] = sums[t]
                if both:
                    ref = out.pop(0)
                    for t in range(2):
                        ref[t, h] = sums[t].astype(LOW)
                for j in range(selects):
                    ref = out.pop(0)
                    ref[h] = jnp.where(flags_ref[j] != 0, sums[1], sums[0]).astype(LOW)
            if reach is not None:
                sides = []
                for t in range(2):
                    value = None if around_ref is None else around_ref[t, h]
                    for p, part in enumerate(got):
                        term = weight(reach[p][t]) * part[t]
                        value = term if value is None else value + term
                    sides.append(value)
                if final is None:
                    ref = out.pop(0)
                    for t in range(2):
                        ref[t, h] = sides[t]
                else:
                    for i, ref in enumerate(out):
                        for t in range(2):
                            value = sides[t]
                            if extra_refs:
                                a, b = final[4 * i + 2 * t : 4 * i + 2 * t + 2]
                                value = weight(a) * value + weight(b) * extra_refs[i][
                                    t, h
                                ].astype(WIDE)
                            ref[t, h] = value.astype(LOW)

    def block(x):
        if len(x.shape) == 3:
            return pl.BlockSpec((hs, HEAD_DIM, HEAD_DIM), lambda i, *_: (i, 0, 0))
        return pl.BlockSpec((2, hs, HEAD_DIM, HEAD_DIM), lambda i, *_: (0, i, 0, 0))

    return order.call(
        kernel,
        "step",
        [table, flags],
        inputs,
        [block(x) for x in inputs],
        out_shape,
        [block(x) for x in out_shape],
        grid=(hw // hs,),
    )


def grads(order, cols, pieces, group, decay, st, outs, full, w0, hw, hb):
    _, _, rows, _ = pieces[0].shape
    count = len(pieces)
    span = count * rows
    width = hb * HEAD_DIM
    aliased = outs is not None
    cumr, weights, bias = decay
    n_in = count + 4

    def kernel(cols_ref, *refs):
        got = refs[:count]
        w_ref, cumr_ref, bias_ref, st_ref = refs[count:n_in]
        results = refs[n_in + (3 if aliased else 0) :]
        kept, sends = results[:3], results[3:]
        for h in range(hb):
            c = head_cols(h)
            q, k, v, g = (
                jnp.concatenate([r[0, a, :, c] for r in got], axis=0) for a in range(4)
            )
            cumc, qw, kw = (
                w_ref[0, 0, :, j * hb + h : j * hb + h + 1] for j in range(3)
            )
            outputs = head_grads(
                q, k, v, g, qw, kw, cumc,
                cumr_ref[0, 0, h : h + 1, :], bias_ref[...], st_ref[0, h], st_ref[1, h],
            )
            for a, result in enumerate(outputs):
                kept[a][:, c] = result[:rows]
                for m, send in enumerate(sends):
                    send[a, :, c] = result[(m + 1) * rows : (m + 2) * rows]

    piece = pl.BlockSpec((1, 4, rows, width), lambda i, c: (group, 0, 0, i))
    column = pl.BlockSpec((1, 1, span, 3 * hb), lambda i, c: (w0 // hb + i, group, 0, 0))
    row = pl.BlockSpec((1, 1, hb, span), lambda i, c: (w0 // hb + i, group, 0, 0))
    whole = pl.BlockSpec((span, span), lambda i, c: (0, 0))
    state_block = pl.BlockSpec((2, hb, HEAD_DIM, HEAD_DIM), lambda i, c: (0, i, 0, 0))
    results = order.call(
        kernel,
        "grads",
        [cols],
        [*pieces, weights, cumr, bias, st] + (list(outs) if aliased else []),
        [piece] * count
        + [column, row, whole, state_block]
        + ([ANY] * 3 if aliased else []),
        [jax.ShapeDtypeStruct((rows, full), LOW)] * 3
        + [jax.ShapeDtypeStruct((3, rows, hw * HEAD_DIM), LOW)] * (count - 1),
        [pl.BlockSpec((rows, width), lambda i, c: (0, c[group] + i))] * 3
        + [pl.BlockSpec((3, rows, width), lambda i, c: (0, 0, i))] * (count - 1),
        grid=(hw // hb,),
        aliases={1 + n_in + a: a for a in range(3)} if aliased else {},
    )
    return (results[:3], results[3:])


def place(order, ats, parts, outs):
    rows, full = outs[0].shape
    count = len(parts)

    def kernel(at_ref, *refs):
        ins, results, sems = refs[:count], refs[count + 3 : count + 6], refs[count + 6]
        copies = []
        for p, ref in enumerate(ins):
            columns = pl.ds(pl.multiple_of(at_ref[p] * HEAD_DIM, HEAD_DIM), ref.shape[2])
            for a in range(3):
                copies.append(
                    pltpu.make_async_copy(
                        ref.at[a], results[a].at[:, columns], sems.at[len(copies)]
                    )
                )
        for copy in copies:
            copy.start()
        for copy in copies:
            copy.wait()

    return order.call(
        kernel,
        "place",
        [jnp.stack(ats)],
        [*parts, *outs],
        [FULL] * count + [ANY] * 3,
        [jax.ShapeDtypeStruct((rows, full), LOW)] * 3,
        [ANY] * 3,
        scratch=[pltpu.SemaphoreType.DMA((3 * count,))],
        aliases={1 + count + a: a for a in range(3)},
    )


class Table:
    def __init__(self, log_decay, low):
        self.peers = lax.axis_size("seq")
        self.me = lax.axis_index("seq")
        sums = jnp.sum(log_decay.reshape(log_decay.shape[0], 2, -1), axis=2)
        self.lo, self.hi, self.on, self.gate = [], [], [], []
        self.sums = sums
        every = (sums[:, 0] + sums[:, 1])[None]
        bit = 1
        while bit < self.peers:
            other = swap(every, "seq", bit)
            late = (self.me & bit) != 0
            every = jnp.where(
                late,
                jnp.concatenate([other, every], axis=0),
                jnp.concatenate([every, other], axis=0),
            )
            bit *= 2
        self.every = jnp.concatenate([every, sums.T], axis=0)

    def row(self, a, b, on=True):
        self.lo.append(jnp.asarray(a, jnp.int32))
        self.hi.append(jnp.asarray(b, jnp.int32))
        self.on.append(jnp.asarray(on, jnp.bool_))
        return len(self.lo) - 1

    def one_if(self, on):
        return self.row(0, 0, on)

    def half_if(self, which, use):
        at = self.peers + which
        return self.row(jnp.where(use, at, 0), jnp.where(use, at + 1, 0))

    def build(self):
        index = jnp.arange(self.peers + 2)[None, :]
        inside = (index >= jnp.stack(self.lo)[:, None]) & (index < jnp.stack(self.hi)[:, None])
        total = jnp.sum(jnp.where(inside[:, :, None], self.every[None], 0.0), axis=1)
        return jnp.where(jnp.stack(self.on)[:, None], jnp.exp(total), 0.0)


def seq_levels(table):
    bits = table.peers.bit_length() - 1
    me = table.me
    levels = []
    base = 0
    while base < bits:
        nb = min(1 if base == 0 else 2, bits - base)
        size = 1 << base
        start = me - me % size
        above = me - me % (size << nb)
        end = above + (size << nb)
        last = base + nb == bits
        level = dict(base=base, nb=nb, last=last, reach=[], add=[], keep=None)
        if not last:
            level["keep"] = (table.row(start + size, end), table.row(above, start))
        for p in range(1, 1 << nb):
            other = start ^ (p << base)
            level["reach"].append(
                (
                    table.row(other + size, me, other < start),
                    table.row(me + 1, other, other > start),
                )
            )
            if not last:
                level["add"].append((table.row(other + size, end), table.row(above, other)))
        levels.append(level)
        base += nb
    return levels


class Wave:
    def __init__(self, env, mode, w0, hw):
        self.env, self.mode, self.w0, self.hw = env, mode, w0, hw
        self.peers = range(1, env.n // 2 if mode == "P" else env.n)
        self.parts = []

    def columns(self, device):
        at = [device, device ^ (self.env.n // 2)] if self.mode == "P" else [device]
        return (jnp.stack(at) * self.env.heads + self.w0).astype(jnp.int32)

    def pack(self):
        e = self.env
        self.received = [None] * len(self.peers)
        for m in sorted(self.peers, reverse=True):
            first = pack_away if self.w0 == 0 else pack
            packed = first(e.order, self.columns(e.z ^ m), e.arrays, self.hw)
            self.received[m - 1] = swap(packed, "head", m)

    def keep(self):
        e = self.env
        self.kept = pack(e.order, self.columns(e.z), e.arrays, self.hw)
        self.pieces = [self.kept] + self.received

    def states(self):
        e = self.env
        self.decay = e.decay[self.mode]
        self.level = 0
        self.around = None
        self.own, *send = states(e.order, self.pieces, self.decay, self.w0, self.hw, e.hb)
        if send:
            self.theirs = swap(send[0], "head", e.n // 2)

    def begin(self):
        e = self.env
        levels = e.levels
        if not levels:
            return
        level = levels[0]
        result = step(
            e.order, e.table, e.flags, self.w0, self.hw, self.own,
            [self.theirs] if self.mode == "P" else [], None,
            keep=e.comb[0] if self.mode == "P" else e.ones,
            add=[e.comb[1]] if self.mode == "P" else [],
            total=not level["last"], both=not level["last"],
            selects=level["nb"] if level["last"] else 0,
        )
        self.exchange(result, level)

    def exchange(self, result, level):
        if level["last"]:
            sends = result
        else:
            self.total = result[0]
            sends = [result[1]]
        self.got = []
        for p in range(1, 1 << level["nb"]):
            send = sends[p.bit_length() - 1] if level["last"] else sends[0]
            self.got.append(swap(send, "seq", p << level["base"]))

    def advance(self):
        e = self.env
        level, after = e.levels[self.level], e.levels[self.level + 1]
        result = step(
            e.order, e.table, e.flags, self.w0, self.hw, self.total, self.got, self.around,
            keep=level["keep"], add=level["add"], reach=level["reach"],
            total=not after["last"], both=not after["last"],
            selects=after["nb"] if after["last"] else 0,
        )
        self.around = result.pop()
        self.level += 1
        self.exchange(result, after)

    def finish(self):
        e = self.env
        level = e.levels[-1] if e.levels else None
        zero = jnp.zeros((2, self.hw, HEAD_DIM, HEAD_DIM), WIDE)
        result = step(
            e.order, e.table, e.flags, self.w0, self.hw, None,
            self.got if level else [], self.around if level and len(e.levels) > 1 else zero,
            reach=level["reach"] if level else [], single=True,
            final=e.final if self.mode == "P" else e.ones * 2,
            extras=[self.theirs, self.own] if self.mode == "P" else [],
        )
        self.own_states = result[0]
        if self.mode == "P":
            self.mirror_states = swap(result[1], "head", e.n // 2)

    def touch(self):
        self.env.order.call(lambda *refs: None, "touch", [], [self.mirror_states], [ANY], [], [])

    def arrive(self):
        e = self.env
        count = len(self.received)
        e.order.call(lambda *refs: None, "arrive", [], self.received, [ANY] * count, [], [])

    def grads(self, group):
        e = self.env
        st = self.mirror_states if group else self.own_states
        e.outs, sends = grads(
            e.order, self.columns(e.z) // e.hb, self.pieces, group, self.decay, st, e.outs,
            e.arrays[0].shape[1], self.w0, self.hw, e.hb,
        )
        for m in sorted(self.peers, reverse=True):
            at = self.columns(e.z ^ m)[group]
            self.parts.append((at, swap(sends[m - 1], "head", m)))

    def place(self):
        e = self.env
        if self.parts:
            e.outs = place(
                e.order, [t[0] for t in self.parts], [t[1] for t in self.parts], e.outs
            )
            self.parts = []


class Env:
    pass


def local(queries, key_rows, value_rows, out_grad, log_decay):
    e = Env()
    e.arrays = (queries, key_rows, value_rows, out_grad)
    rows = queries.shape[0]
    e.heads = heads = log_decay.shape[0]
    e.hb = math.gcd(heads, PART)
    e.n = n = lax.axis_size("head")
    e.z = z = lax.axis_index("head")
    e.order = Order()
    e.outs = None
    e.decay = {}
    half = n // 2
    low = z < half

    def prepare(modes):
        table = Table(log_decay, low)
        e.levels = seq_levels(table)
        e.ones = (table.one_if(True),) * 2
        e.comb = (
            (table.half_if(1, low), table.half_if(0, ~low)),
            (table.half_if(1, ~low), table.half_if(0, low)),
        )
        off, on = table.one_if(~low), table.one_if(low)
        e.final = (
            table.half_if(0, ~low), off, table.half_if(1, low), on,
            table.half_if(0, low), on, table.half_if(1, ~low), off,
        )
        e.table = table.build()
        top = e.levels[-1] if e.levels else dict(base=0, nb=1)
        e.flags = jnp.stack(
            [(table.me >> (top["base"] + j)) & 1 for j in range(top["nb"])]
        ).astype(jnp.int32)
        if "P" in modes:
            at = jnp.stack([z % half, z // half]).astype(jnp.int32)
            mirror = swap(log_decay, "head", half)
            e.decay["P"] = decays(e.order, at, [log_decay, mirror], rows, half, e.hb)
        if "X" in modes:
            at = jnp.stack([z, z * 0]).astype(jnp.int32)
            e.decay["X"] = decays(e.order, at, [log_decay], rows, n, e.hb)

    schedule(e, heads, prepare)
    return tuple(e.outs)


WAVES = ("P8", "P8")
STEPS = ("pa", "pb", "ua", "x", "ka", "sa", "kb", "sb", "ba", "va", "fa", "bb", "vb", "ga", "ta", "fb", "gb", "la", "ha", "hb", "la", "lb")


def schedule(e, heads, prepare):
    sizes, steps = WAVES, STEPS
    if heads % 16:
        sizes, steps = ("P16",), ("pa", "x", "ka", "sa", "ba", "va", "fa", "ga", "ha", "la")
    waves, w0 = {}, 0
    for name, size in zip("abcdef", sizes):
        hw = int(size[1:]) * heads // 16
        waves[name] = Wave(e, size[0], w0, hw)
        w0 += hw
    for code in steps:
        if code == "x":
            prepare({size[0] for size in sizes})
            continue
        wave = waves[code[1]]
        if code[0] == "p":
            wave.pack()
        elif code[0] == "k":
            wave.keep()
        elif code[0] == "s":
            wave.states()
        elif code[0] == "b":
            wave.begin()
        elif code[0] == "v":
            for _ in e.levels[1:]:
                wave.advance()
        elif code[0] == "f":
            wave.finish()
        elif code[0] == "g":
            wave.grads(0)
        elif code[0] == "h":
            wave.grads(1)
        elif code[0] == "l":
            wave.place()
        elif code[0] == "t":
            wave.touch()
        elif code[0] == "u":
            wave.arrive()


def solution(mesh):
    rows = P(("seq", "head"), None)
    return jax.shard_map(
        local,
        mesh=mesh,
        in_specs=(rows, rows, rows, rows, P("head", "seq")),
        out_specs=(rows, rows, rows),
        check_vma=False,
    )
```

```python
import functools
import math

import jax
import jax.numpy as jnp
from jax import lax
from jax.experimental import pallas as pl
from jax.experimental.pallas import tpu as pltpu
from jax.sharding import PartitionSpec as P

HEAD_DIM = 128
PART = 4
STEP = 8
VMEM = 16 * 1024 * 1024
ANY = pl.BlockSpec(memory_space=pl.ANY)
FULL = pl.BlockSpec(memory_space=pltpu.VMEM)
SCALARS = pl.BlockSpec(memory_space=pltpu.SMEM)
NN = ((1,), (0,))
NT = ((1,), (1,))
TN = ((0,), (0,))
LOW = jnp.bfloat16
COST = pl.CostEstimate(flops=1, bytes_accessed=1, transcendentals=0)
TOUCH_COST = pl.CostEstimate(flops=1, bytes_accessed=1, transcendentals=0)
GRADS_COST = pl.CostEstimate(flops=4000000000, bytes_accessed=1, transcendentals=0)
WIDE = jnp.float32


def swap(x, axis, bit):
    return lax.ppermute(x, axis, [(i, i ^ bit) for i in range(lax.axis_size(axis))])


def dot(a, b, dims):
    return lax.dot_general(a, b, (dims, ((), ())), preferred_element_type=WIDE)


def head_cols(h):
    return slice(h * HEAD_DIM, (h + 1) * HEAD_DIM)


class Order:
    def __init__(self):
        self.token = None

    def call(
        self,
        kernel,
        name,
        scalars,
        inputs,
        in_specs,
        out_shape,
        out_specs,
        grid=(),
        scratch=(),
        aliases=None,
        after=(),
        vmem=VMEM,
    ):
        extra = list(after) + ([] if self.token is None else [self.token])
        n_scalars, n_in, n_out = len(scalars), len(inputs), len(out_shape)

        def body(*refs):
            first = n_scalars + n_in
            second = first + len(extra)
            kernel(*refs[:first], *refs[second : second + n_out], *refs[second + n_out + 1 :])

        *results, self.token = pl.pallas_call(
            body,
            grid_spec=pltpu.PrefetchScalarGridSpec(
                num_scalar_prefetch=n_scalars,
                grid=grid,
                in_specs=list(in_specs) + [ANY] * len(extra),
                out_specs=list(out_specs) + [ANY],
                scratch_shapes=scratch,
            ),
            out_shape=list(out_shape) + [jax.ShapeDtypeStruct((8, 128), WIDE)],
            input_output_aliases=aliases or {},
            compiler_params=pltpu.CompilerParams(vmem_limit_bytes=vmem),
            cost_estimate={"grads": GRADS_COST, "touch": TOUCH_COST}.get(name, COST),
            name=name,
        )(*scalars, *inputs, *extra)
        return results


def head_states(q, k, v, g, qw, kw):
    ks = (k.astype(WIDE) * kw).astype(LOW)
    qs = (q.astype(WIDE) * qw).astype(LOW)
    return dot(ks, v, TN), dot(qs, g, TN)


def head_grads(q, k, v, g, qw, kw, cumc, cumr, bias, forward, backward):
    decay = jnp.exp(cumc - cumr + bias)
    gs = (dot(g, v, NT) * decay).astype(LOW)
    sc = (dot(q, k, NT) * decay).astype(LOW)
    dq = dot(gs, k, NN) + qw * dot(g, forward, NT)
    dk = dot(gs, q, TN) + kw * dot(v, backward, NT)
    dv = dot(sc, g, TN) + kw * dot(k, backward, NN)
    return dq.astype(LOW), dk.astype(LOW), dv.astype(LOW)


def pack(order, target, arrays, hw):
    rows = arrays[0].shape[0]
    width = hw * HEAD_DIM
    groups = target.shape[0]

    def kernel(at_ref, *refs):
        ins, out, sems = refs[:4], refs[4], refs[5]
        copies = []
        for o in range(groups):
            columns = pl.ds(pl.multiple_of(at_ref[o] * HEAD_DIM, HEAD_DIM), width)
            for a, ref in enumerate(ins):
                copies.append(
                    pltpu.make_async_copy(
                        ref.at[:, columns], out.at[o, a], sems.at[len(copies)]
                    )
                )
        for copy in copies:
            copy.start()
        for copy in copies:
            copy.wait()

    (packed,) = order.call(
        kernel,
        "pack",
        [target],
        arrays,
        [pl.BlockSpec(memory_space=pltpu.HBM)] * 4,
        [jax.ShapeDtypeStruct((groups, 4, rows, width), LOW)],
        [FULL],
        scratch=[pltpu.SemaphoreType.DMA((4 * groups,))],
    )
    return packed


def pack_away(order, wave, m, arrays, hw):
    rows = arrays[0].shape[0]
    width = hw * HEAD_DIM
    groups = 2
    half, heads, w0 = wave.env.n // 2, wave.env.heads, wave.w0
    shape = (groups, 4, rows, width)

    def kernel(*refs):
        device = lax.axis_index("head") ^ m
        ins, out, buffer, sems = refs[:4], refs[4], refs[5], refs[6]
        loads, stores = [], []
        for o in range(groups):
            columns = pl.ds(pl.multiple_of(((device ^ (o * half)) * heads + w0) * HEAD_DIM, HEAD_DIM), width)
            for a, ref in enumerate(ins):
                n = len(loads)
                loads.append(
                    pltpu.make_async_copy(ref.at[:, columns], buffer.at[o, a], sems.at[0, n])
                )
                stores.append(
                    pltpu.make_async_copy(buffer.at[o, a], out.at[o, a], sems.at[1, n])
                )
        for load in loads:
            load.start()
        for load, store in zip(loads, stores):
            load.wait()
            store.start()
        for store in stores:
            store.wait()

    (packed,) = order.call(
        kernel,
        "pack",
        [],
        arrays,
        [ANY] * 4,
        [jax.ShapeDtypeStruct(shape, LOW)],
        [ANY],
        scratch=[pltpu.VMEM(shape, LOW), pltpu.SemaphoreType.DMA((2, 4 * groups))],
        vmem=60 * 1024 * 1024,
    )
    return packed


def decays(order, at, logs, rows, pieces, hb):
    heads, length = logs[0].shape
    span = pieces * rows
    groups = len(logs)
    steps = heads // hb

    def kernel(at_ref, *refs):
        sources = refs[:groups]
        cumr, cols, bias = refs[groups:]
        slot, upper = at_ref[0], at_ref[1]

        def position(axis):
            p = lax.broadcasted_iota(jnp.int32, (span, span), axis)
            return ((p // rows) ^ slot) * rows + p % rows

        down, along = position(0), position(1)
        bias[...] = jnp.where(down >= along, 0.0, -1e30)
        source = lax.broadcasted_iota(jnp.int32, (span, span), 0)
        upto = (source <= along).astype(WIDE)
        ones = jnp.ones((span, span), WIDE)
        for o, ref in enumerate(sources):
            rows_in = ref[...]
            if span < length:
                rows_in = jnp.where(upper == 0, rows_in[:, :span], rows_in[:, span:])

            def exact(a, b, dims):
                return lax.dot_general(
                    a,
                    b,
                    (dims, ((), ())),
                    precision=lax.Precision.HIGHEST,
                    preferred_element_type=WIDE,
                )

            line = exact(rows_in, upto, NN)
            column = exact(upto, rows_in, ((0,), (1,)))
            total = exact(ones, rows_in, NT)
            query = jnp.exp(column)
            key = jnp.exp(total - column)
            for i in range(steps):
                part = slice(i * hb, (i + 1) * hb)
                cumr[i, o] = line[part]
                for j, value in enumerate((column, query, key)):
                    cols[i, o, :, j * hb : (j + 1) * hb] = value[:, part]

    columns = jax.ShapeDtypeStruct((steps, groups, span, 3 * hb), WIDE)
    return order.call(
        kernel,
        "decays",
        [at],
        logs,
        [FULL] * groups,
        [
            jax.ShapeDtypeStruct((steps, groups, hb, span), WIDE),
            columns,
            jax.ShapeDtypeStruct((span, span), WIDE),
        ],
        [FULL] * 3,
    )


def states(order, pieces, decay, w0, hw, hb):
    groups, _, rows, _ = pieces[0].shape
    count = len(pieces)
    width = hb * HEAD_DIM

    def kernel(*refs):
        got = refs[:count]
        cols_ref, *results = refs[count:]
        for o in range(groups):
            for h in range(hb):
                c = head_cols(h)
                q, k, v, g = (
                    jnp.concatenate([r[o, a, :, c] for r in got], axis=0) for a in range(4)
                )
                qw = cols_ref[0, o, :, hb + h : hb + h + 1]
                kw = cols_ref[0, o, :, 2 * hb + h : 2 * hb + h + 1]
                pair = head_states(q, k, v, g, qw, kw)
                for t in range(2):
                    results[o][t, h] = pair[t].astype(results[o].dtype)

    piece = pl.BlockSpec((groups, 4, rows, width), lambda i: (0, 0, 0, i))
    weight = pl.BlockSpec((1, groups, count * rows, 3 * hb), lambda i: (w0 // hb + i, 0, 0, 0))
    shape = (2, hw, HEAD_DIM, HEAD_DIM)
    return order.call(
        kernel,
        "states",
        [],
        [*pieces, decay[1]],
        [piece] * count + [weight],
        [jax.ShapeDtypeStruct(shape, kind) for kind in (WIDE, LOW)[:groups]],
        [pl.BlockSpec((2, hb, HEAD_DIM, HEAD_DIM), lambda i: (0, i, 0, 0))] * groups,
        grid=(hw // hb,),
    )


def step(order, table, flags, w0, hw, own, parts, around, keep=None, add=None, reach=None,
         single=False, both=False, selects=0, total=False, final=None, extras=()):
    shape = (2, hw, HEAD_DIM, HEAD_DIM)
    hs = math.gcd(hw, STEP)
    inputs = ([] if own is None else [own]) + list(parts)
    inputs += ([] if around is None else [around]) + list(extras)
    out_shape = []
    if total:
        out_shape.append(jax.ShapeDtypeStruct(shape, WIDE))
    if both:
        out_shape.append(jax.ShapeDtypeStruct(shape, LOW))
    out_shape += [jax.ShapeDtypeStruct(shape[1:], LOW)] * selects
    if reach is not None and final is None:
        out_shape.append(jax.ShapeDtypeStruct(shape, WIDE))
    if final is not None:
        out_shape += [jax.ShapeDtypeStruct(shape, LOW)] * (len(final) // 4)

    def kernel(table_ref, flags_ref, *refs):
        refs = list(refs)
        own_ref = None if own is None else refs.pop(0)
        part_refs = [refs.pop(0) for _ in parts]
        around_ref = None if around is None else refs.pop(0)
        extra_refs = [refs.pop(0) for _ in extras]

        first = w0 + pl.program_id(0) * hs

        for h in range(hs):
            out = list(refs)

            def weight(row):
                return table_ref[row, first + h]

            got = [
                [r[h].astype(WIDE)] * 2 if single else [r[t, h].astype(WIDE) for t in range(2)]
                for r in part_refs
            ]
            if keep is not None:
                sums = []
                for t in range(2):
                    value = weight(keep[t]) * own_ref[t, h]
                    for p, part in enumerate(got):
                        value = value + weight(add[p][t]) * part[t]
                    sums.append(value)
                if total:
                    ref = out.pop(0)
                    for t in range(2):
                        ref[t, h] = sums[t]
                if both:
                    ref = out.pop(0)
                    for t in range(2):
                        ref[t, h] = sums[t].astype(LOW)
                for j in range(selects):
                    ref = out.pop(0)
                    ref[h] = jnp.where(flags_ref[j] != 0, sums[1], sums[0]).astype(LOW)
            if reach is not None:
                sides = []
                for t in range(2):
                    value = None if around_ref is None else around_ref[t, h]
                    for p, part in enumerate(got):
                        term = weight(reach[p][t]) * part[t]
                        value = term if value is None else value + term
                    sides.append(value)
                if final is None:
                    ref = out.pop(0)
                    for t in range(2):
                        ref[t, h] = sides[t]
                else:
                    for i, ref in enumerate(out):
                        for t in range(2):
                            value = sides[t]
                            if extra_refs:
                                a, b = final[4 * i + 2 * t : 4 * i + 2 * t + 2]
                                value = weight(a) * value + weight(b) * extra_refs[i][
                                    t, h
                                ].astype(WIDE)
                            ref[t, h] = value.astype(LOW)

    def block(x):
        if len(x.shape) == 3:
            return pl.BlockSpec((hs, HEAD_DIM, HEAD_DIM), lambda i, *_: (i, 0, 0))
        return pl.BlockSpec((2, hs, HEAD_DIM, HEAD_DIM), lambda i, *_: (0, i, 0, 0))

    return order.call(
        kernel,
        "step",
        [table, flags],
        inputs,
        [block(x) for x in inputs],
        out_shape,
        [block(x) for x in out_shape],
        grid=(hw // hs,),
    )


def grads(order, cols, pieces, group, decay, st, outs, full, w0, hw, hb):
    _, _, rows, _ = pieces[0].shape
    count = len(pieces)
    span = count * rows
    width = hb * HEAD_DIM
    aliased = outs is not None
    cumr, weights, bias = decay
    n_in = count + 4

    def kernel(cols_ref, *refs):
        got = refs[:count]
        w_ref, cumr_ref, bias_ref, st_ref = refs[count:n_in]
        results = refs[n_in + (3 if aliased else 0) :]
        kept, sends = results[:3], results[3:]
        for h in range(hb):
            c = head_cols(h)
            q, k, v, g = (
                jnp.concatenate([r[0, a, :, c] for r in got], axis=0) for a in range(4)
            )
            cumc, qw, kw = (
                w_ref[0, 0, :, j * hb + h : j * hb + h + 1] for j in range(3)
            )
            outputs = head_grads(
                q, k, v, g, qw, kw, cumc,
                cumr_ref[0, 0, h : h + 1, :], bias_ref[...], st_ref[0, h], st_ref[1, h],
            )
            for a, result in enumerate(outputs):
                kept[a][:, c] = result[:rows]
                for m, send in enumerate(sends):
                    send[a, :, c] = result[(m + 1) * rows : (m + 2) * rows]

    piece = pl.BlockSpec((1, 4, rows, width), lambda i, c: (group, 0, 0, i))
    column = pl.BlockSpec((1, 1, span, 3 * hb), lambda i, c: (w0 // hb + i, group, 0, 0))
    row = pl.BlockSpec((1, 1, hb, span), lambda i, c: (w0 // hb + i, group, 0, 0))
    whole = pl.BlockSpec((span, span), lambda i, c: (0, 0))
    state_block = pl.BlockSpec((2, hb, HEAD_DIM, HEAD_DIM), lambda i, c: (0, i, 0, 0))
    results = order.call(
        kernel,
        "grads",
        [cols],
        [*pieces, weights, cumr, bias, st] + (list(outs) if aliased else []),
        [piece] * count
        + [column, row, whole, state_block]
        + ([ANY] * 3 if aliased else []),
        [jax.ShapeDtypeStruct((rows, full), LOW)] * 3
        + [jax.ShapeDtypeStruct((3, rows, hw * HEAD_DIM), LOW)] * (count - 1),
        [pl.BlockSpec((rows, width), lambda i, c: (0, c[group] + i))] * 3
        + [pl.BlockSpec((3, rows, width), lambda i, c: (0, 0, i))] * (count - 1),
        grid=(hw // hb,),
        aliases={1 + n_in + a: a for a in range(3)} if aliased else {},
    )
    return (results[:3], results[3:])


def place(order, ats, parts, outs):
    rows, full = outs[0].shape
    count = len(parts)

    def kernel(at_ref, *refs):
        ins, results, sems = refs[:count], refs[count + 3 : count + 6], refs[count + 6]
        copies = []
        for p, ref in enumerate(ins):
            columns = pl.ds(pl.multiple_of(at_ref[p] * HEAD_DIM, HEAD_DIM), ref.shape[2])
            for a in range(3):
                copies.append(
                    pltpu.make_async_copy(
                        ref.at[a], results[a].at[:, columns], sems.at[len(copies)]
                    )
                )
        for copy in copies:
            copy.start()
        for copy in copies:
            copy.wait()

    return order.call(
        kernel,
        "place",
        [jnp.stack(ats)],
        [*parts, *outs],
        [FULL] * count + [ANY] * 3,
        [jax.ShapeDtypeStruct((rows, full), LOW)] * 3,
        [ANY] * 3,
        scratch=[pltpu.SemaphoreType.DMA((3 * count,))],
        aliases={1 + count + a: a for a in range(3)},
    )


class Table:
    def __init__(self, log_decay, low):
        self.peers = lax.axis_size("seq")
        self.me = lax.axis_index("seq")
        sums = jnp.sum(log_decay.reshape(log_decay.shape[0], 2, -1), axis=2)
        self.lo, self.hi, self.on, self.gate = [], [], [], []
        self.sums = sums
        every = (sums[:, 0] + sums[:, 1])[None]
        bit = 1
        while bit < self.peers:
            other = swap(every, "seq", bit)
            late = (self.me & bit) != 0
            every = jnp.where(
                late,
                jnp.concatenate([other, every], axis=0),
                jnp.concatenate([every, other], axis=0),
            )
            bit *= 2
        self.every = jnp.concatenate([every, sums.T], axis=0)

    def row(self, a, b, on=True):
        self.lo.append(jnp.asarray(a, jnp.int32))
        self.hi.append(jnp.asarray(b, jnp.int32))
        self.on.append(jnp.asarray(on, jnp.bool_))
        return len(self.lo) - 1

    def one_if(self, on):
        return self.row(0, 0, on)

    def half_if(self, which, use):
        at = self.peers + which
        return self.row(jnp.where(use, at, 0), jnp.where(use, at + 1, 0))

    def build(self):
        index = jnp.arange(self.peers + 2)[None, :]
        inside = (index >= jnp.stack(self.lo)[:, None]) & (index < jnp.stack(self.hi)[:, None])
        total = jnp.sum(jnp.where(inside[:, :, None], self.every[None], 0.0), axis=1)
        return jnp.where(jnp.stack(self.on)[:, None], jnp.exp(total), 0.0)


def seq_levels(table):
    bits = table.peers.bit_length() - 1
    me = table.me
    levels = []
    base = 0
    while base < bits:
        nb = min(1 if base == 0 else 2, bits - base)
        size = 1 << base
        start = me - me % size
        above = me - me % (size << nb)
        end = above + (size << nb)
        last = base + nb == bits
        level = dict(base=base, nb=nb, last=last, reach=[], add=[], keep=None)
        if not last:
            level["keep"] = (table.row(start + size, end), table.row(above, start))
        for p in range(1, 1 << nb):
            other = start ^ (p << base)
            level["reach"].append(
                (
                    table.row(other + size, me, other < start),
                    table.row(me + 1, other, other > start),
                )
            )
            if not last:
                level["add"].append((table.row(other + size, end), table.row(above, other)))
        levels.append(level)
        base += nb
    return levels


class Wave:
    def __init__(self, env, mode, w0, hw):
        self.env, self.mode, self.w0, self.hw = env, mode, w0, hw
        self.peers = range(1, env.n // 2 if mode == "P" else env.n)
        self.parts = []

    def columns(self, device):
        at = [device, device ^ (self.env.n // 2)] if self.mode == "P" else [device]
        return (jnp.stack(at) * self.env.heads + self.w0).astype(jnp.int32)

    def pack(self):
        e = self.env
        self.received = [None] * len(self.peers)
        for m in sorted(self.peers, reverse=True):
            if self.w0 == 0:
                packed = pack_away(e.order, self, m, e.arrays, self.hw)
            else:
                packed = pack(e.order, self.columns(e.z ^ m), e.arrays, self.hw)
            self.received[m - 1] = swap(packed, "head", m)

    def keep(self):
        e = self.env
        self.kept = pack(e.order, self.columns(e.z), e.arrays, self.hw)
        self.pieces = [self.kept] + self.received

    def states(self):
        e = self.env
        self.decay = e.decay[self.mode]
        self.level = 0
        self.around = None
        self.own, *send = states(e.order, self.pieces, self.decay, self.w0, self.hw, e.hb)
        if send:
            self.theirs = swap(send[0], "head", e.n // 2)

    def begin(self):
        e = self.env
        levels = e.levels
        if not levels:
            return
        level = levels[0]
        result = step(
            e.order, e.table, e.flags, self.w0, self.hw, self.own,
            [self.theirs] if self.mode == "P" else [], None,
            keep=e.comb[0] if self.mode == "P" else e.ones,
            add=[e.comb[1]] if self.mode == "P" else [],
            total=not level["last"], both=not level["last"],
            selects=level["nb"] if level["last"] else 0,
        )
        self.exchange(result, level)

    def exchange(self, result, level):
        if level["last"]:
            sends = result
        else:
            self.total = result[0]
            sends = [result[1]]
        self.got = []
        for p in range(1, 1 << level["nb"]):
            send = sends[p.bit_length() - 1] if level["last"] else sends[0]
            self.got.append(swap(send, "seq", p << level["base"]))

    def advance(self):
        e = self.env
        level, after = e.levels[self.level], e.levels[self.level + 1]
        result = step(
            e.order, e.table, e.flags, self.w0, self.hw, self.total, self.got, self.around,
            keep=level["keep"], add=level["add"], reach=level["reach"],
            total=not after["last"], both=not after["last"],
            selects=after["nb"] if after["last"] else 0,
        )
        self.around = result.pop()
        self.level += 1
        self.exchange(result, after)

    def finish(self):
        e = self.env
        level = e.levels[-1] if e.levels else None
        zero = jnp.zeros((2, self.hw, HEAD_DIM, HEAD_DIM), WIDE)
        result = step(
            e.order, e.table, e.flags, self.w0, self.hw, None,
            self.got if level else [], self.around if level and len(e.levels) > 1 else zero,
            reach=level["reach"] if level else [], single=True,
            final=e.final if self.mode == "P" else e.ones * 2,
            extras=[self.theirs, self.own] if self.mode == "P" else [],
        )
        self.own_states = result[0]
        if self.mode == "P":
            self.mirror_states = swap(result[1], "head", e.n // 2)

    def touch(self):
        self.env.order.call(lambda *refs: None, "touch", [], [self.mirror_states], [ANY], [], [])

    def arrive(self):
        e = self.env
        count = len(self.received)
        e.order.call(lambda *refs: None, "arrive", [], self.received, [ANY] * count, [], [])

    def grads(self, group):
        e = self.env
        st = self.mirror_states if group else self.own_states
        e.outs, sends = grads(
            e.order, self.columns(e.z) // e.hb, self.pieces, group, self.decay, st, e.outs,
            e.arrays[0].shape[1], self.w0, self.hw, e.hb,
        )
        for m in sorted(self.peers, reverse=True):
            at = self.columns(e.z ^ m)[group]
            self.parts.append((at, swap(sends[m - 1], "head", m)))

    def place(self):
        e = self.env
        if self.parts:
            e.outs = place(
                e.order, [t[0] for t in self.parts], [t[1] for t in self.parts], e.outs
            )
            self.parts = []


class Env:
    pass


def local(queries, key_rows, value_rows, out_grad, log_decay):
    e = Env()
    e.arrays = (queries, key_rows, value_rows, out_grad)
    rows = queries.shape[0]
    e.heads = heads = log_decay.shape[0]
    e.hb = math.gcd(heads, PART)
    e.n = n = lax.axis_size("head")
    e.z = z = lax.axis_index("head")
    e.order = Order()
    e.outs = None
    e.decay = {}
    half = n // 2
    low = z < half

    def prepare(modes):
        table = Table(log_decay, low)
        e.levels = seq_levels(table)
        e.ones = (table.one_if(True),) * 2
        e.comb = (
            (table.half_if(1, low), table.half_if(0, ~low)),
            (table.half_if(1, ~low), table.half_if(0, low)),
        )
        off, on = table.one_if(~low), table.one_if(low)
        e.final = (
            table.half_if(0, ~low), off, table.half_if(1, low), on,
            table.half_if(0, low), on, table.half_if(1, ~low), off,
        )
        e.table = table.build()
        top = e.levels[-1] if e.levels else dict(base=0, nb=1)
        e.flags = jnp.stack(
            [(table.me >> (top["base"] + j)) & 1 for j in range(top["nb"])]
        ).astype(jnp.int32)
        if "P" in modes:
            at = jnp.stack([z % half, z // half]).astype(jnp.int32)
            mirror = swap(log_decay, "head", half)
            e.decay["P"] = decays(e.order, at, [log_decay, mirror], rows, half, e.hb)
        if "X" in modes:
            at = jnp.stack([z, z * 0]).astype(jnp.int32)
            e.decay["X"] = decays(e.order, at, [log_decay], rows, n, e.hb)

    schedule(e, heads, prepare)
    return tuple(e.outs)


WAVES = ("P8", "P8")
STEPS = ("pa", "pb", "ua", "x", "ka", "sa", "kb", "sb", "ba", "va", "fa", "bb", "vb", "ga", "ta", "fb", "gb", "la", "ha", "hb", "la", "lb")


def schedule(e, heads, prepare):
    sizes, steps = WAVES, STEPS
    if heads % 16:
        sizes, steps = ("P16",), ("pa", "x", "ka", "sa", "ba", "va", "fa", "ga", "ha", "la")
    waves, w0 = {}, 0
    for name, size in zip("abcdef", sizes):
        hw = int(size[1:]) * heads // 16
        waves[name] = Wave(e, size[0], w0, hw)
        w0 += hw
    for code in steps:
        if code == "x":
            prepare({size[0] for size in sizes})
            continue
        wave = waves[code[1]]
        if code[0] == "p":
            wave.pack()
        elif code[0] == "k":
            wave.keep()
        elif code[0] == "s":
            wave.states()
        elif code[0] == "b":
            wave.begin()
        elif code[0] == "v":
            for _ in e.levels[1:]:
                wave.advance()
        elif code[0] == "f":
            wave.finish()
        elif code[0] == "g":
            wave.grads(0)
        elif code[0] == "h":
            wave.grads(1)
        elif code[0] == "l":
            wave.place()
        elif code[0] == "t":
            wave.touch()
        elif code[0] == "u":
            wave.arrive()


def solution(mesh):
    rows = P(("seq", "head"), None)
    return jax.shard_map(
        local,
        mesh=mesh,
        in_specs=(rows, rows, rows, rows, P("head", "seq")),
        out_specs=(rows, rows, rows),
        check_vma=False,
    )
```

```python
import functools
import math

import jax
import jax.numpy as jnp
from jax import lax
from jax.experimental import pallas as pl
from jax.experimental.pallas import tpu as pltpu
from jax.sharding import PartitionSpec as P

HEAD_DIM = 128
PART = 4
STEP = 8
VMEM = 16 * 1024 * 1024
ANY = pl.BlockSpec(memory_space=pl.ANY)
FULL = pl.BlockSpec(memory_space=pltpu.VMEM)
SCALARS = pl.BlockSpec(memory_space=pltpu.SMEM)
NN = ((1,), (0,))
NT = ((1,), (1,))
TN = ((0,), (0,))
LOW = jnp.bfloat16
COST = pl.CostEstimate(flops=1, bytes_accessed=1, transcendentals=0)
TOUCH_COST = pl.CostEstimate(flops=1, bytes_accessed=1, transcendentals=0)
GRADS_COST = pl.CostEstimate(flops=4000000000, bytes_accessed=1, transcendentals=0)
WIDE = jnp.float32


def swap(x, axis, bit):
    return lax.ppermute(x, axis, [(i, i ^ bit) for i in range(lax.axis_size(axis))])


def dot(a, b, dims):
    return lax.dot_general(a, b, (dims, ((), ())), preferred_element_type=WIDE)


def head_cols(h):
    return slice(h * HEAD_DIM, (h + 1) * HEAD_DIM)


class Order:
    def __init__(self):
        self.token = None

    def call(
        self,
        kernel,
        name,
        scalars,
        inputs,
        in_specs,
        out_shape,
        out_specs,
        grid=(),
        scratch=(),
        aliases=None,
        after=(),
        vmem=VMEM,
    ):
        extra = list(after) + ([] if self.token is None else [self.token])
        n_scalars, n_in, n_out = len(scalars), len(inputs), len(out_shape)

        def body(*refs):
            first = n_scalars + n_in
            second = first + len(extra)
            kernel(*refs[:first], *refs[second : second + n_out], *refs[second + n_out + 1 :])

        *results, self.token = pl.pallas_call(
            body,
            grid_spec=pltpu.PrefetchScalarGridSpec(
                num_scalar_prefetch=n_scalars,
                grid=grid,
                in_specs=list(in_specs) + [ANY] * len(extra),
                out_specs=list(out_specs) + [ANY],
                scratch_shapes=scratch,
            ),
            out_shape=list(out_shape) + [jax.ShapeDtypeStruct((8, 128), WIDE)],
            input_output_aliases=aliases or {},
            compiler_params=pltpu.CompilerParams(vmem_limit_bytes=vmem),
            cost_estimate={"grads": GRADS_COST, "touch": TOUCH_COST}.get(name, COST),
            name=name,
        )(*scalars, *inputs, *extra)
        return results


def head_states(q, k, v, g, qw, kw):
    ks = (k.astype(WIDE) * kw).astype(LOW)
    qs = (q.astype(WIDE) * qw).astype(LOW)
    return dot(ks, v, TN), dot(qs, g, TN)


def head_grads(q, k, v, g, qw, kw, cumc, cumr, bias, forward, backward):
    decay = jnp.exp(cumc - cumr + bias)
    gs = (dot(g, v, NT) * decay).astype(LOW)
    sc = (dot(q, k, NT) * decay).astype(LOW)
    dq = dot(gs, k, NN) + qw * dot(g, forward, NT)
    dk = dot(gs, q, TN) + kw * dot(v, backward, NT)
    dv = dot(sc, g, TN) + kw * dot(k, backward, NN)
    return dq.astype(LOW), dk.astype(LOW), dv.astype(LOW)


def pack(order, target, arrays, hw):
    rows = arrays[0].shape[0]
    width = hw * HEAD_DIM
    groups = target.shape[0]

    def kernel(at_ref, *refs):
        ins, out, sems = refs[:4], refs[4], refs[5]
        copies = []
        for o in range(groups):
            columns = pl.ds(pl.multiple_of(at_ref[o] * HEAD_DIM, HEAD_DIM), width)
            for a, ref in enumerate(ins):
                copies.append(
                    pltpu.make_async_copy(
                        ref.at[:, columns], out.at[o, a], sems.at[len(copies)]
                    )
                )
        for copy in copies:
            copy.start()
        for copy in copies:
            copy.wait()

    (packed,) = order.call(
        kernel,
        "pack",
        [target],
        arrays,
        [pl.BlockSpec(memory_space=pltpu.HBM)] * 4,
        [jax.ShapeDtypeStruct((groups, 4, rows, width), LOW)],
        [FULL],
        scratch=[pltpu.SemaphoreType.DMA((4 * groups,))],
    )
    return packed


def pack_away(order, wave, m, arrays, hw):
    rows = arrays[0].shape[0]
    width = hw * HEAD_DIM
    groups = 2
    half, heads, w0 = wave.env.n // 2, wave.env.heads, wave.w0
    shape = (groups, 4, rows, width)

    def kernel(*refs):
        device = lax.axis_index("head") ^ m
        ins, out, buffer, sems = refs[:4], refs[4], refs[5], refs[6]
        loads, stores = [], []
        for o in range(groups):
            columns = pl.ds(pl.multiple_of(((device ^ (o * half)) * heads + w0) * HEAD_DIM, HEAD_DIM), width)
            for a, ref in enumerate(ins):
                n = len(loads)
                loads.append(
                    pltpu.make_async_copy(ref.at[:, columns], buffer.at[o, a], sems.at[0, n])
                )
                stores.append(
                    pltpu.make_async_copy(buffer.at[o, a], out.at[o, a], sems.at[1, n])
                )
        for load in loads:
            load.start()
        for load, store in zip(loads, stores):
            load.wait()
            store.start()
        for store in stores:
            store.wait()

    (packed,) = order.call(
        kernel,
        "pack",
        [],
        arrays,
        [ANY] * 4,
        [jax.ShapeDtypeStruct(shape, LOW)],
        [ANY],
        scratch=[pltpu.VMEM(shape, LOW), pltpu.SemaphoreType.DMA((2, 4 * groups))],
        vmem=60 * 1024 * 1024,
    )
    return packed


def decays(order, at, logs, rows, pieces, hb):
    heads, length = logs[0].shape
    span = pieces * rows
    groups = len(logs)
    steps = heads // hb

    def kernel(at_ref, *refs):
        sources = refs[:groups]
        cumr, cols, bias = refs[groups:]
        slot, upper = at_ref[0], at_ref[1]

        def position(axis):
            p = lax.broadcasted_iota(jnp.int32, (span, span), axis)
            return ((p // rows) ^ slot) * rows + p % rows

        down, along = position(0), position(1)
        bias[...] = jnp.where(down >= along, 0.0, -1e30)
        source = lax.broadcasted_iota(jnp.int32, (span, span), 0)
        upto = (source <= along).astype(WIDE)
        ones = jnp.ones((span, span), WIDE)
        for o, ref in enumerate(sources):
            rows_in = ref[...]
            if span < length:
                rows_in = jnp.where(upper == 0, rows_in[:, :span], rows_in[:, span:])

            def exact(a, b, dims):
                return lax.dot_general(
                    a,
                    b,
                    (dims, ((), ())),
                    precision=lax.Precision.HIGHEST,
                    preferred_element_type=WIDE,
                )

            line = exact(rows_in, upto, NN)
            column = exact(upto, rows_in, ((0,), (1,)))
            total = exact(ones, rows_in, NT)
            query = jnp.exp(column)
            key = jnp.exp(total - column)
            for i in range(steps):
                part = slice(i * hb, (i + 1) * hb)
                cumr[i, o] = line[part]
                for j, value in enumerate((column, query, key)):
                    cols[i, o, :, j * hb : (j + 1) * hb] = value[:, part]

    columns = jax.ShapeDtypeStruct((steps, groups, span, 3 * hb), WIDE)
    return order.call(
        kernel,
        "decays",
        [at],
        logs,
        [FULL] * groups,
        [
            jax.ShapeDtypeStruct((steps, groups, hb, span), WIDE),
            columns,
            jax.ShapeDtypeStruct((span, span), WIDE),
        ],
        [FULL] * 3,
    )


def states(order, pieces, decay, w0, hw, hb):
    groups, _, rows, _ = pieces[0].shape
    count = len(pieces)
    width = hb * HEAD_DIM

    def kernel(*refs):
        got = refs[:count]
        cols_ref, *results = refs[count:]
        for o in range(groups):
            for h in range(hb):
                c = head_cols(h)
                q, k, v, g = (
                    jnp.concatenate([r[o, a, :, c] for r in got], axis=0) for a in range(4)
                )
                qw = cols_ref[0, o, :, hb + h : hb + h + 1]
                kw = cols_ref[0, o, :, 2 * hb + h : 2 * hb + h + 1]
                pair = head_states(q, k, v, g, qw, kw)
                for t in range(2):
                    results[o][t, h] = pair[t].astype(results[o].dtype)

    piece = pl.BlockSpec((groups, 4, rows, width), lambda i: (0, 0, 0, i))
    weight = pl.BlockSpec((1, groups, count * rows, 3 * hb), lambda i: (w0 // hb + i, 0, 0, 0))
    shape = (2, hw, HEAD_DIM, HEAD_DIM)
    return order.call(
        kernel,
        "states",
        [],
        [*pieces, decay[1]],
        [piece] * count + [weight],
        [jax.ShapeDtypeStruct(shape, kind) for kind in (WIDE, LOW)[:groups]],
        [pl.BlockSpec((2, hb, HEAD_DIM, HEAD_DIM), lambda i: (0, i, 0, 0))] * groups,
        grid=(hw // hb,),
    )


def step(order, table, flags, w0, hw, own, parts, around, keep=None, add=None, reach=None,
         single=False, both=False, selects=0, total=False, final=None, extras=()):
    shape = (2, hw, HEAD_DIM, HEAD_DIM)
    hs = math.gcd(hw, STEP)
    inputs = ([] if own is None else [own]) + list(parts)
    inputs += ([] if around is None else [around]) + list(extras)
    out_shape = []
    if total:
        out_shape.append(jax.ShapeDtypeStruct(shape, WIDE))
    if both:
        out_shape.append(jax.ShapeDtypeStruct(shape, LOW))
    out_shape += [jax.ShapeDtypeStruct(shape[1:], LOW)] * selects
    if reach is not None and final is None:
        out_shape.append(jax.ShapeDtypeStruct(shape, WIDE))
    if final is not None:
        out_shape += [jax.ShapeDtypeStruct(shape, LOW)] * (len(final) // 4)

    def kernel(table_ref, flags_ref, *refs):
        refs = list(refs)
        own_ref = None if own is None else refs.pop(0)
        part_refs = [refs.pop(0) for _ in parts]
        around_ref = None if around is None else refs.pop(0)
        extra_refs = [refs.pop(0) for _ in extras]

        first = w0 + pl.program_id(0) * hs

        for h in range(hs):
            out = list(refs)

            def weight(row):
                return table_ref[row, first + h]

            got = [
                [r[h].astype(WIDE)] * 2 if single else [r[t, h].astype(WIDE) for t in range(2)]
                for r in part_refs
            ]
            if keep is not None:
                sums = []
                for t in range(2):
                    value = weight(keep[t]) * own_ref[t, h]
                    for p, part in enumerate(got):
                        value = value + weight(add[p][t]) * part[t]
                    sums.append(value)
                if total:
                    ref = out.pop(0)
                    for t in range(2):
                        ref[t, h] = sums[t]
                if both:
                    ref = out.pop(0)
                    for t in range(2):
                        ref[t, h] = sums[t].astype(LOW)
                for j in range(selects):
                    ref = out.pop(0)
                    ref[h] = jnp.where(flags_ref[j] != 0, sums[1], sums[0]).astype(LOW)
            if reach is not None:
                sides = []
                for t in range(2):
                    value = None if around_ref is None else around_ref[t, h]
                    for p, part in enumerate(got):
                        term = weight(reach[p][t]) * part[t]
                        value = term if value is None else value + term
                    sides.append(value)
                if final is None:
                    ref = out.pop(0)
                    for t in range(2):
                        ref[t, h] = sides[t]
                else:
                    for i, ref in enumerate(out):
                        for t in range(2):
                            value = sides[t]
                            if extra_refs:
                                a, b = final[4 * i + 2 * t : 4 * i + 2 * t + 2]
                                value = weight(a) * value + weight(b) * extra_refs[i][
                                    t, h
                                ].astype(WIDE)
                            ref[t, h] = value.astype(LOW)

    def block(x):
        if len(x.shape) == 3:
            return pl.BlockSpec((hs, HEAD_DIM, HEAD_DIM), lambda i, *_: (i, 0, 0))
        return pl.BlockSpec((2, hs, HEAD_DIM, HEAD_DIM), lambda i, *_: (0, i, 0, 0))

    return order.call(
        kernel,
        "step",
        [table, flags],
        inputs,
        [block(x) for x in inputs],
        out_shape,
        [block(x) for x in out_shape],
        grid=(hw // hs,),
    )


def grads(order, cols, pieces, group, decay, st, outs, full, w0, hw, hb):
    _, _, rows, _ = pieces[0].shape
    count = len(pieces)
    span = count * rows
    width = hb * HEAD_DIM
    aliased = outs is not None
    cumr, weights, bias = decay
    n_in = count + 4

    def kernel(cols_ref, *refs):
        got = refs[:count]
        w_ref, cumr_ref, bias_ref, st_ref = refs[count:n_in]
        results = refs[n_in + (3 if aliased else 0) :]
        kept, sends = results[:3], results[3:]
        for h in range(hb):
            c = head_cols(h)
            q, k, v, g = (
                jnp.concatenate([r[0, a, :, c] for r in got], axis=0) for a in range(4)
            )
            cumc, qw, kw = (
                w_ref[0, 0, :, j * hb + h : j * hb + h + 1] for j in range(3)
            )
            outputs = head_grads(
                q, k, v, g, qw, kw, cumc,
                cumr_ref[0, 0, h : h + 1, :], bias_ref[...], st_ref[0, h], st_ref[1, h],
            )
            for a, result in enumerate(outputs):
                kept[a][:, c] = result[:rows]
                for m, send in enumerate(sends):
                    send[a, :, c] = result[(m + 1) * rows : (m + 2) * rows]

    piece = pl.BlockSpec((1, 4, rows, width), lambda i, c: (group, 0, 0, i))
    column = pl.BlockSpec((1, 1, span, 3 * hb), lambda i, c: (w0 // hb + i, group, 0, 0))
    row = pl.BlockSpec((1, 1, hb, span), lambda i, c: (w0 // hb + i, group, 0, 0))
    whole = pl.BlockSpec((span, span), lambda i, c: (0, 0))
    state_block = pl.BlockSpec((2, hb, HEAD_DIM, HEAD_DIM), lambda i, c: (0, i, 0, 0))
    results = order.call(
        kernel,
        "grads",
        [cols],
        [*pieces, weights, cumr, bias, st] + (list(outs) if aliased else []),
        [piece] * count
        + [column, row, whole, state_block]
        + ([ANY] * 3 if aliased else []),
        [jax.ShapeDtypeStruct((rows, full), LOW)] * 3
        + [jax.ShapeDtypeStruct((3, rows, hw * HEAD_DIM), LOW)] * (count - 1),
        [pl.BlockSpec((rows, width), lambda i, c: (0, c[group] + i))] * 3
        + [pl.BlockSpec((3, rows, width), lambda i, c: (0, 0, i))] * (count - 1),
        grid=(hw // hb,),
        aliases={1 + n_in + a: a for a in range(3)} if aliased else {},
    )
    return (results[:3], results[3:])


def place(order, ats, parts, outs):
    rows, full = outs[0].shape
    count = len(parts)

    def kernel(at_ref, *refs):
        ins, results, sems = refs[:count], refs[count + 3 : count + 6], refs[count + 6]
        copies = []
        for p, ref in enumerate(ins):
            columns = pl.ds(pl.multiple_of(at_ref[p] * HEAD_DIM, HEAD_DIM), ref.shape[2])
            for a in range(3):
                copies.append(
                    pltpu.make_async_copy(
                        ref.at[a], results[a].at[:, columns], sems.at[len(copies)]
                    )
                )
        for copy in copies:
            copy.start()
        for copy in copies:
            copy.wait()

    return order.call(
        kernel,
        "place",
        [jnp.stack(ats)],
        [*parts, *outs],
        [FULL] * count + [ANY] * 3,
        [jax.ShapeDtypeStruct((rows, full), LOW)] * 3,
        [ANY] * 3,
        scratch=[pltpu.SemaphoreType.DMA((3 * count,))],
        aliases={1 + count + a: a for a in range(3)},
    )


class Table:
    def __init__(self, log_decay, low):
        self.peers = lax.axis_size("seq")
        self.me = lax.axis_index("seq")
        sums = jnp.sum(log_decay.reshape(log_decay.shape[0], 2, -1), axis=2)
        self.lo, self.hi, self.on, self.gate = [], [], [], []
        self.sums = sums
        every = (sums[:, 0] + sums[:, 1])[None]
        bit = 1
        while bit < self.peers:
            other = swap(every, "seq", bit)
            late = (self.me & bit) != 0
            every = jnp.where(
                late,
                jnp.concatenate([other, every], axis=0),
                jnp.concatenate([every, other], axis=0),
            )
            bit *= 2
        self.every = jnp.concatenate([every, sums.T], axis=0)

    def row(self, a, b, on=True):
        self.lo.append(jnp.asarray(a, jnp.int32))
        self.hi.append(jnp.asarray(b, jnp.int32))
        self.on.append(jnp.asarray(on, jnp.bool_))
        return len(self.lo) - 1

    def one_if(self, on):
        return self.row(0, 0, on)

    def half_if(self, which, use):
        at = self.peers + which
        return self.row(jnp.where(use, at, 0), jnp.where(use, at + 1, 0))

    def build(self):
        index = jnp.arange(self.peers + 2)[None, :]
        inside = (index >= jnp.stack(self.lo)[:, None]) & (index < jnp.stack(self.hi)[:, None])
        total = jnp.sum(jnp.where(inside[:, :, None], self.every[None], 0.0), axis=1)
        return jnp.where(jnp.stack(self.on)[:, None], jnp.exp(total), 0.0)


def seq_levels(table):
    bits = table.peers.bit_length() - 1
    me = table.me
    levels = []
    base = 0
    while base < bits:
        nb = min(1 if base == 0 else 2, bits - base)
        size = 1 << base
        start = me - me % size
        above = me - me % (size << nb)
        end = above + (size << nb)
        last = base + nb == bits
        level = dict(base=base, nb=nb, last=last, reach=[], add=[], keep=None)
        if not last:
            level["keep"] = (table.row(start + size, end), table.row(above, start))
        for p in range(1, 1 << nb):
            other = start ^ (p << base)
            level["reach"].append(
                (
                    table.row(other + size, me, other < start),
                    table.row(me + 1, other, other > start),
                )
            )
            if not last:
                level["add"].append((table.row(other + size, end), table.row(above, other)))
        levels.append(level)
        base += nb
    return levels


class Wave:
    def __init__(self, env, mode, w0, hw):
        self.env, self.mode, self.w0, self.hw = env, mode, w0, hw
        self.peers = range(1, env.n // 2 if mode == "P" else env.n)
        self.parts = []

    def columns(self, device):
        at = [device, device ^ (self.env.n // 2)] if self.mode == "P" else [device]
        return (jnp.stack(at) * self.env.heads + self.w0).astype(jnp.int32)

    def pack(self):
        e = self.env
        self.received = [None] * len(self.peers)
        for m in sorted(self.peers, reverse=True):
            if self.w0 == 0:
                packed = pack_away(e.order, self, m, e.arrays, self.hw)
            else:
                packed = pack(e.order, self.columns(e.z ^ m), e.arrays, self.hw)
            self.received[m - 1] = swap(packed, "head", m)

    def keep(self):
        e = self.env
        self.kept = pack(e.order, self.columns(e.z), e.arrays, self.hw)
        self.pieces = [self.kept] + self.received

    def states(self):
        e = self.env
        self.decay = e.decay[self.mode]
        self.level = 0
        self.around = None
        self.own, *send = states(e.order, self.pieces, self.decay, self.w0, self.hw, e.hb)
        if send:
            self.theirs = swap(send[0], "head", e.n // 2)

    def begin(self):
        e = self.env
        levels = e.levels
        if not levels:
            return
        level = levels[0]
        result = step(
            e.order, e.table, e.flags, self.w0, self.hw, self.own,
            [self.theirs] if self.mode == "P" else [], None,
            keep=e.comb[0] if self.mode == "P" else e.ones,
            add=[e.comb[1]] if self.mode == "P" else [],
            total=not level["last"], both=not level["last"],
            selects=level["nb"] if level["last"] else 0,
        )
        self.exchange(result, level)

    def exchange(self, result, level):
        if level["last"]:
            sends = result
        else:
            self.total = result[0]
            sends = [result[1]]
        self.got = [None] * ((1 << level["nb"]) - 1)
        for p in reversed(range(1, 1 << level["nb"])):
            send = sends[p.bit_length() - 1] if level["last"] else sends[0]
            self.got[p - 1] = swap(send, "seq", p << level["base"])

    def advance(self):
        e = self.env
        level, after = e.levels[self.level], e.levels[self.level + 1]
        result = step(
            e.order, e.table, e.flags, self.w0, self.hw, self.total, self.got, self.around,
            keep=level["keep"], add=level["add"], reach=level["reach"],
            total=not after["last"], both=not after["last"],
            selects=after["nb"] if after["last"] else 0,
        )
        self.around = result.pop()
        self.level += 1
        self.exchange(result, after)

    def finish(self):
        e = self.env
        level = e.levels[-1] if e.levels else None
        zero = jnp.zeros((2, self.hw, HEAD_DIM, HEAD_DIM), WIDE)
        result = step(
            e.order, e.table, e.flags, self.w0, self.hw, None,
            self.got if level else [], self.around if level and len(e.levels) > 1 else zero,
            reach=level["reach"] if level else [], single=True,
            final=e.final if self.mode == "P" else e.ones * 2,
            extras=[self.theirs, self.own] if self.mode == "P" else [],
        )
        self.own_states = result[0]
        if self.mode == "P":
            self.mirror_states = swap(result[1], "head", e.n // 2)

    def touch(self):
        self.env.order.call(lambda *refs: None, "touch", [], [self.mirror_states], [ANY], [], [])

    def arrive(self):
        e = self.env
        count = len(self.received)
        e.order.call(lambda *refs: None, "arrive", [], self.received, [ANY] * count, [], [])

    def grads(self, group):
        e = self.env
        st = self.mirror_states if group else self.own_states
        e.outs, sends = grads(
            e.order, self.columns(e.z) // e.hb, self.pieces, group, self.decay, st, e.outs,
            e.arrays[0].shape[1], self.w0, self.hw, e.hb,
        )
        for m in sorted(self.peers, reverse=True):
            at = self.columns(e.z ^ m)[group]
            self.parts.append((at, swap(sends[m - 1], "head", m)))

    def place(self):
        e = self.env
        if self.parts:
            e.outs = place(
                e.order, [t[0] for t in self.parts], [t[1] for t in self.parts], e.outs
            )
            self.parts = []


class Env:
    pass


def local(queries, key_rows, value_rows, out_grad, log_decay):
    e = Env()
    e.arrays = (queries, key_rows, value_rows, out_grad)
    rows = queries.shape[0]
    e.heads = heads = log_decay.shape[0]
    e.hb = math.gcd(heads, PART)
    e.n = n = lax.axis_size("head")
    e.z = z = lax.axis_index("head")
    e.order = Order()
    e.outs = None
    e.decay = {}
    half = n // 2
    low = z < half

    def prepare(modes):
        table = Table(log_decay, low)
        e.levels = seq_levels(table)
        e.ones = (table.one_if(True),) * 2
        e.comb = (
            (table.half_if(1, low), table.half_if(0, ~low)),
            (table.half_if(1, ~low), table.half_if(0, low)),
        )
        off, on = table.one_if(~low), table.one_if(low)
        e.final = (
            table.half_if(0, ~low), off, table.half_if(1, low), on,
            table.half_if(0, low), on, table.half_if(1, ~low), off,
        )
        e.table = table.build()
        top = e.levels[-1] if e.levels else dict(base=0, nb=1)
        e.flags = jnp.stack(
            [(table.me >> (top["base"] + j)) & 1 for j in range(top["nb"])]
        ).astype(jnp.int32)
        if "P" in modes:
            at = jnp.stack([z % half, z // half]).astype(jnp.int32)
            mirror = swap(log_decay, "head", half)
            e.decay["P"] = decays(e.order, at, [log_decay, mirror], rows, half, e.hb)
        if "X" in modes:
            at = jnp.stack([z, z * 0]).astype(jnp.int32)
            e.decay["X"] = decays(e.order, at, [log_decay], rows, n, e.hb)

    schedule(e, heads, prepare)
    return tuple(e.outs)


WAVES = ("P8", "P8")
STEPS = ("pa", "pb", "ua", "x", "ka", "sa", "kb", "sb", "ba", "va", "fa", "bb", "vb", "ga", "ta", "fb", "gb", "la", "ha", "hb", "la", "lb")


def schedule(e, heads, prepare):
    sizes, steps = WAVES, STEPS
    if heads % 16:
        sizes, steps = ("P16",), ("pa", "x", "ka", "sa", "ba", "va", "fa", "ga", "ha", "la")
    waves, w0 = {}, 0
    for name, size in zip("abcdef", sizes):
        hw = int(size[1:]) * heads // 16
        waves[name] = Wave(e, size[0], w0, hw)
        w0 += hw
    for code in steps:
        if code == "x":
            prepare({size[0] for size in sizes})
            continue
        wave = waves[code[1]]
        if code[0] == "p":
            wave.pack()
        elif code[0] == "k":
            wave.keep()
        elif code[0] == "s":
            wave.states()
        elif code[0] == "b":
            wave.begin()
        elif code[0] == "v":
            for _ in e.levels[1:]:
                wave.advance()
        elif code[0] == "f":
            wave.finish()
        elif code[0] == "g":
            wave.grads(0)
        elif code[0] == "h":
            wave.grads(1)
        elif code[0] == "l":
            wave.place()
        elif code[0] == "t":
            wave.touch()
        elif code[0] == "u":
            wave.arrive()


def solution(mesh):
    rows = P(("seq", "head"), None)
    return jax.shard_map(
        local,
        mesh=mesh,
        in_specs=(rows, rows, rows, rows, P("head", "seq")),
        out_specs=(rows, rows, rows),
        check_vma=False,
    )
```
